256 devices in a mesh: dom: 16 (over z, core), sub: 16 (over x, y).
Axes of the slice: x: 4, y: 4, z: 8, core: 2. Of those that a mesh axis runs over, the one named last changes fastest.
Arguments:
- a_blocks: bfloat16 [21504, 7, 64, 64], P(('dom', 'sub')), may hold values from -0.75 to 0.75
- a_cols: int32 [21504, 7], P(('dom', 'sub')), may hold values from 0 to 21503, as said below
- p_blocks: bfloat16 [21504, 3, 64, 64], P(('dom', 'sub')), may hold values from -0.75 to 0.75
- p_cols: int32 [21504, 3], P(('dom', 'sub')), may hold values from 0 to 6143, as said below
- c_cols: int32 [6144, 8], P(('dom', 'sub')), may hold values from 0 to 6143, as said below
Outputs:
- coarse_blocks: bfloat16 [6144, 8, 64, 64], P(('dom', 'sub'))
The draws below stay inside these ranges and needn't reach their ends.
Inputs may be any that keep to these rules, and one draw needn't show every extreme that they name: a_cols[i,0] is i; the entries of a row are distinct; each is a fine block row held by the device of row i, by the device with the next or previous dom index and the same sub index, or by the device with the next or previous sub index and the same dom index (indices wrap around). Rows of the device with the next dom index read only rows of aggregate set 6 - 1 of this device, rows of the device with the previous dom index only rows of set 6 - 2, the device with the next sub index only the rows whose prolongator columns lie on it, the device with the previous sub index only rows of sets 0 and 1; set of a row here means its coarse columns' aggregate set. `p_cols`: the 3 entries of a row are distinct coarse block rows of one aggregate set, the rows 4 * j to 4 * j + 3 for some j; they are owned by the device of the fine row, or they are the first 4 coarse rows owned by the device with the next sub index and the same dom index (wrapping around); each device holds 14 fine rows of each of its sets 1 to 5, half of 14 of its set 0, and half of 14 rows of the next sub device's set 0. A row holds 8 distinct coarse block rows: the 4 rows of its own aggregate set, then the 4 rows of one other set; all rows of one aggregate set list the same 8 coarse rows, in any order; for all i, k, p, q the coarse row p_cols[a_cols[i,k], q] appears in row p_cols[i,p] of c_cols.
All inputs are finite; a program needn't handle non-finite values.
Results may differ from the reference program's by a relative error of at most 0.0054.
Values may be sent and summed in bfloat16 or wider, within the bound.
No kernel may reach another device: no remote copies, remote signals or barrier semaphores. Data moves between devices by JAX's collectives and lax.ppermute only.
A program may use at most 256 MiB of HBM per device.

```python
import jax
import jax.numpy as jnp
from jax import lax

B = 64
KA = 7
KP = 3
KG = 4
FS = 14
NG = 6
CB = 24
KC = 8
RB = 84
NB = 21504
NC = 6144
N_DOM = 16
N_SUB = 16


def layout(key):
    subkeys = jax.random.split(key, 5)
    devices_all = N_DOM * N_SUB
    half = FS // 2
    device_ids = jnp.arange(devices_all, dtype=jnp.int32)
    dom_of = device_ids // N_SUB
    sub_of = device_ids % N_SUB
    shuffles = jax.vmap(lambda subkey: jax.random.permutation(subkey, RB))(jax.random.split(subkeys[0], devices_all)).astype(jnp.int32)
    set_ids = jnp.arange(NG, dtype=jnp.int32)
    slot_ids = jnp.arange(FS, dtype=jnp.int32)
    prev_sub = dom_of * N_SUB + (sub_of - 1) % N_SUB
    straddle = (set_ids[:, None] == 0) & (slot_ids[None, :] < half)
    holder = jnp.where(straddle[None, :, :], prev_sub[:, None, None], device_ids[:, None, None])
    canon = jnp.broadcast_to((set_ids[:, None] * FS + slot_ids[None, :])[None, :, :], (devices_all, NG, FS))
    row_id = holder * RB + shuffles[holder, canon]
    next_dom = (dom_of + 1) % N_DOM * N_SUB + sub_of
    prev_dom = (dom_of - 1) % N_DOM * N_SUB + sub_of
    set_grid = jnp.broadcast_to(set_ids[None, :], (devices_all, NG))
    pair_set = set_grid + 1 - 2 * (set_grid % 2)
    mate_dev = jnp.where(set_grid == NG - 1, next_dom[:, None], jnp.where(set_grid == NG - 2, prev_dom[:, None], device_ids[:, None]))
    mate_set = jnp.where(set_grid == NG - 1, NG - 2, jnp.where(set_grid == NG - 2, NG - 1, pair_set))
    mate_rows = row_id[mate_dev, mate_set]
    own_index = (slot_ids[:, None] + jnp.arange(4, dtype=jnp.int32)[None, :]) % FS
    own_pick = row_id[:, :, own_index]
    turn = jax.random.randint(subkeys[1], (devices_all, NG, 1, 1), 0, FS)
    mate_index = (slot_ids[None, None, :, None] + turn + jnp.arange(KA - 4, dtype=jnp.int32)[None, None, None, :]) % FS
    wide_mates = jnp.broadcast_to(mate_rows[:, :, None, :], (devices_all, NG, FS, FS))
    mate_pick = jnp.take_along_axis(wide_mates, mate_index, axis=3)
    a_role = jnp.concatenate([own_pick, mate_pick], axis=3)
    skipped = jax.random.randint(subkeys[2], (devices_all, NG, FS, 1), 0, KG)
    picked = (skipped + 1 + jnp.arange(KP, dtype=jnp.int32)) % KG
    p_role = device_ids[:, None, None, None] * CB + set_ids[None, :, None, None] * KG + picked
    rows_flat = row_id.reshape(-1)
    a_table = jnp.zeros((NB, KA), jnp.int32).at[rows_flat].set(a_role.reshape(-1, KA))
    p_table = jnp.zeros((NB, KP), jnp.int32).at[rows_flat].set(p_role.reshape(-1, KP))
    member_ids = jnp.arange(KG, dtype=jnp.int32)
    turn_own = jax.random.randint(subkeys[3], (devices_all, NG, KG, 1), 0, KG)
    turn_mate = jax.random.randint(subkeys[4], (devices_all, NG, KG, 1), 0, KG)
    own_list = device_ids[:, None, None, None] * CB + set_ids[None, :, None, None] * KG + (member_ids + turn_own) % KG
    mate_list = mate_dev[:, :, None, None] * CB + mate_set[:, :, None, None] * KG + (member_ids + turn_mate) % KG
    c_table = jnp.concatenate([own_list, mate_list], axis=3).reshape(NC, KC)
    return (a_table, p_table, c_table)


def draw_a_cols(key, part):
    tables = layout(key)
    return tables[0]


def draw_p_cols(key, part):
    tables = layout(key)
    return tables[1]


def draw_c_cols(key, part):
    tables = layout(key)
    return tables[2]


def levels(own_key, extent, cuts, low, largest):
    def one(dim, blocks):
        draws = jax.random.uniform(jax.random.fold_in(jax.random.fold_in(own_key, 6), dim), (blocks,), jnp.float32, low / len(cuts), largest / len(cuts))
        return jnp.repeat(jnp.exp(draws), extent[dim] // blocks).reshape((-1,) + (1,) * (len(extent) - dim - 1))

    level = one(*cuts[0])
    for cut in cuts[1:]:
        level = level * one(*cut)
    return level


def normal_values(rng, extent, scale, bound, shards=(), kind=jnp.bfloat16):
    entries = scale * jax.random.normal(rng, extent, jnp.float32)
    if shards:
        entries = entries * levels(rng, extent, shards, -0.22, 0.18)
    return jnp.clip(entries, -bound, bound).astype(kind)


def setup_inputs(seed: int = 0) -> dict:
    keys = jax.random.split(jax.random.key(seed), 6)
    a_blocks = normal_values(keys[0], (NB, KA, B, B), B ** -0.5, 0.75, ((0, 256),))
    a_cols = draw_a_cols(jax.random.fold_in(keys[5], 71), 0)
    p_blocks = normal_values(keys[2], (NB, KP, B, B), B ** -0.5, 0.75, ((0, 256),))
    p_cols = draw_p_cols(jax.random.fold_in(keys[5], 71), 0)
    c_cols = draw_c_cols(jax.random.fold_in(keys[5], 71), 0)
    return {"a_blocks": a_blocks, "a_cols": a_cols, "p_blocks": p_blocks, "p_cols": p_cols, "c_cols": c_cols}


def reference(a_blocks, a_cols, p_blocks, p_cols, c_cols):
    def one_device(coarse_sum, device_id):
        first_row = (device_id * RB).astype(jnp.int32)
        a_part = lax.dynamic_slice_in_dim(a_blocks, first_row, RB, 0).astype(jnp.float32)
        columns = lax.dynamic_slice_in_dim(a_cols, first_row, RB, 0)
        p_part = lax.dynamic_slice_in_dim(p_blocks, first_row, RB, 0).astype(jnp.float32)
        rows_coarse = lax.dynamic_slice_in_dim(p_cols, first_row, RB, 0)
        sources = p_blocks[columns].astype(jnp.float32)
        col_coarse = p_cols[columns]
        pattern = c_cols[rows_coarse]
        products = jnp.einsum("ikab,ikqbc->ikqac", a_part, sources, precision=lax.Precision.HIGHEST)
        matched = (col_coarse[:, None, None, :, :] == pattern[:, :, :, None, None]).astype(jnp.float32)
        merged = jnp.einsum("ipskq,ikqac->ipsac", matched, products, precision=lax.Precision.HIGHEST).astype(jnp.bfloat16)
        coarse_terms = jnp.einsum("ipab,ipsac->ipsbc", p_part, merged.astype(jnp.float32), precision=lax.Precision.HIGHEST)
        coarse_sum = coarse_sum.at[rows_coarse.reshape(-1)].add(coarse_terms.reshape((RB * KP, KC, B, B)))
        return coarse_sum, None

    start_sum = jnp.zeros((NC, KC, B, B), jnp.float32)
    coarse_sum, _ = lax.scan(one_device, start_sum, jnp.arange(N_DOM * N_SUB, dtype=jnp.int32))
    return coarse_sum.astype(jnp.bfloat16)
```

```python
import functools

import jax
import jax.numpy as jnp
from jax import lax
from jax.experimental import pallas as pl
from jax.experimental.pallas import tpu as pltpu
from jax.sharding import PartitionSpec as P

KG = 4
FS = 14
HALF = FS // 2
ROWS = 84
PAD = 88
SETS = 6
B = 64
POOL = ROWS + FS + FS + HALF + HALF + FS
F32 = jnp.float32
BF16 = jnp.bfloat16
VMEM_BYTES = 56 * 1024 * 1024


def passed_along(block, axis, distance):
    n = lax.axis_size(axis)
    return lax.ppermute(block, axis, [((i - distance) % n, i) for i in range(n)])


def iota(shape, dim):
    return lax.broadcasted_iota(jnp.int32, shape, dim)


def ranks(lead, set_base):
    group = (lead >> 2) - set_base
    own = (group >= 0) & (group < SETS)
    key = jnp.where(own, jnp.where(group > 0, group + 1, 0), 1)
    order = (key * 128 + iota((1, ROWS), 1)).astype(F32)
    wide = jnp.broadcast_to(order, (ROWS, ROWS))
    diagonal = iota((ROWS, ROWS), 0) == iota((ROWS, ROWS), 1)
    column = jnp.sum(jnp.where(diagonal, wide, 0.0), axis=1, keepdims=True)
    return jnp.sum(jnp.where(column < wide, 1.0, 0.0), axis=0, keepdims=True)


def selector(rank):
    return jnp.where(rank.astype(jnp.int32) == iota((PAD, ROWS), 0), 1.0, 0.0).astype(BF16)


def nt(x, y):
    return lax.dot_general(x, y, (((1,), (1,)), ((), ())), preferred_element_type=F32)


def prolong_kernel(base_ref, cols_ref, p_ref, pool_ref, up_ref, down_ref, fore_ref, back_ref,
                   sel_out_ref, sel_ref, t0_ref, t1_ref):
    @pl.when(pl.program_id(0) == 0)
    def _():
        sel = selector(ranks(cols_ref[0:1, :], base_ref[0]))
        sel_ref[...] = sel
        sel_out_ref[...] = sel

    sel = sel_ref[...]
    place = cols_ref[...] & 3
    weights = [
        [jnp.where(place[q:q + 1, :] == r, 1.0, 0.0).astype(BF16) for q in range(3)]
        for r in range(KG)
    ]
    chunk = p_ref.shape[1]
    for b in range(chunk):
        x = [p_ref[q, b] for q in range(3)]
        y = [x[0] * w[0] + x[1] * w[1] + x[2] * w[2] for w in weights]
        t = nt(sel, jnp.concatenate(y, axis=0))
        t0_ref[b * PAD:(b + 1) * PAD, :] = t[:, :128]
        t1_ref[b * PAD:(b + 1) * PAD, :] = t[:, 128:]
    for i in range(ROWS):
        v = jnp.concatenate(
            [t_ref[pl.ds(i, chunk, stride=PAD), :] for t_ref in (t0_ref, t1_ref)], axis=1
        ).astype(BF16)
        pool_ref[i] = v
        if i >= 70:
            up_ref[i - 70] = v
        elif i >= 56:
            down_ref[i - 56] = v
        elif 7 <= i < 14:
            fore_ref[i - 7] = v
        elif i < 7:
            back_ref[i] = v
        elif i < 28:
            back_ref[i - 7] = v


def prolong(base, cols_t, p_t):
    steps = 4
    chunk = B // steps

    def rows(n):
        return pl.BlockSpec((n, chunk, 4 * B), lambda g: (0, g, 0))

    def shape(n):
        return jax.ShapeDtypeStruct((n, B, 4 * B), BF16)

    return pl.pallas_call(
        prolong_kernel,
        grid=(steps,),
        in_specs=[
            pl.BlockSpec(memory_space=pltpu.SMEM),
            pl.BlockSpec((3, ROWS), lambda g: (0, 0)),
            pl.BlockSpec((3, chunk, B, ROWS), lambda g: (0, g, 0, 0)),
        ],
        out_specs=[rows(84), rows(14), rows(14), rows(7), rows(21),
                   pl.BlockSpec((PAD, ROWS), lambda g: (0, 0))],
        out_shape=[shape(84), shape(14), shape(14), shape(7), shape(21),
                   jax.ShapeDtypeStruct((PAD, ROWS), BF16)],
        scratch_shapes=[
            pltpu.VMEM((PAD, ROWS), BF16),
            pltpu.VMEM((chunk * PAD, 128), F32),
            pltpu.VMEM((chunk * PAD, 128), F32),
        ],
        compiler_params=pltpu.CompilerParams(vmem_limit_bytes=VMEM_BYTES),
        cost_estimate=pl.CostEstimate(flops=400_000_000, bytes_accessed=8_000_000, transcendentals=0),
        name="prolong",
    )(base, cols_t, p_t)


def operator_kernel(sel_ref, a_ref, out_ref, *t_refs):
    sel = sel_ref[...]
    chunk = a_ref.shape[1]
    for a in range(chunk):
        first = jnp.concatenate([a_ref[k, a] for k in range(4)], axis=0)
        zero = jnp.zeros((B, ROWS), BF16)
        last = jnp.concatenate([a_ref[k, a] for k in range(4, 7)] + [zero], axis=0)
        t = [nt(sel, first), nt(sel, last)]
        for h in range(4):
            t_refs[h][a * PAD:(a + 1) * PAD, :] = t[h // 2][:, h % 2 * 128:h % 2 * 128 + 128]
    for i in range(ROWS):
        out_ref[i] = jnp.concatenate(
            [t_ref[pl.ds(i, chunk, stride=PAD), :] for t_ref in t_refs], axis=1
        ).astype(BF16)


def operator(sel, a_t):
    steps = 4
    chunk = B // steps
    return pl.pallas_call(
        operator_kernel,
        grid=(steps,),
        in_specs=[
            pl.BlockSpec((PAD, ROWS), lambda g: (0, 0)),
            pl.BlockSpec((7, chunk, B, ROWS), lambda g: (0, g, 0, 0)),
        ],
        out_specs=pl.BlockSpec((ROWS, chunk, 8 * B), lambda g: (0, g, 0)),
        out_shape=jax.ShapeDtypeStruct((ROWS, B, 8 * B), BF16),
        scratch_shapes=[pltpu.VMEM((chunk * PAD, 128), F32)] * 4,
        compiler_params=pltpu.CompilerParams(vmem_limit_bytes=VMEM_BYTES),
        cost_estimate=pl.CostEstimate(flops=700_000_000, bytes_accessed=13_000_000, transcendentals=0),
        name="operator",
    )(sel, a_t)


def route_kernel(ids_ref, a_cols_ref, own_ref, below_ref, above_ref, before_ref, after_ref,
                 sel_ref, src_ref, mask_ref):
    refs = (own_ref, below_ref, above_ref, before_ref, after_ref)
    rank_rows = [ranks(ref[0:1, :], ids_ref[n] * SETS) for n, ref in enumerate(refs)]
    diagonal = iota((ROWS, ROWS), 0) == iota((ROWS, ROWS), 1)
    after_rank = rank_rows[4]
    rank_rows[1] = rank_rows[1] + (84 - 70)
    rank_rows[2] = rank_rows[2] + (98 - 56)
    rank_rows[3] = rank_rows[3] + (112 - 7)
    rank_rows[4] = after_rank + jnp.where(after_rank < 7, 119.0, 119.0 - 7.0)
    slot_cols = [
        jnp.sum(jnp.where(diagonal, jnp.broadcast_to(r, (ROWS, ROWS)), 0.0), axis=1, keepdims=True)
        for r in rank_rows
    ]
    row = iota((ROWS, ROWS), 0)
    sources = []
    for k in range(7):
        column = a_cols_ref[k:k + 1, :]
        total = jnp.zeros((ROWS, ROWS), F32)
        for n in range(5):
            total = total + jnp.where(column - ids_ref[n] * ROWS == row, slot_cols[n], 0.0)
        sources.append(jnp.sum(total, axis=0, keepdims=True))
    src = jnp.concatenate(sources + [sources[0]], axis=0)

    def set_name(slot):
        name = jnp.where(slot < 7, 0.0, 1.0)
        for start, value in ((14, 2.0), (28, 3.0), (42, 4.0), (56, 5.0), (70, 6.0), (84, 7.0),
                             (98, 8.0), (112, 0.0), (119, 1.0), (126, 9.0)):
            name = jnp.where(slot >= start, value, name)
        return name

    own = jnp.where(set_name(src) == set_name(rank_rows[0]), 1.0, 0.0)
    sel = sel_ref[...]
    src_ref[...] = nt(src.astype(BF16), sel).astype(jnp.int32)
    by_row = nt(sel, own.astype(BF16)).astype(BF16)
    spread = jnp.where(iota((8, 8 * B), 1) >> 6 == iota((8, 8 * B), 0), 1.0, 0.0).astype(BF16)
    mask_ref[...] = jnp.dot(by_row, spread, preferred_element_type=F32)


def route(ids, a_cols_t, cols, sel):
    vmem = pl.BlockSpec(memory_space=pltpu.VMEM)
    return pl.pallas_call(
        route_kernel,
        in_specs=[pl.BlockSpec(memory_space=pltpu.SMEM)] + [vmem] * 7,
        out_specs=[vmem, vmem],
        out_shape=[jax.ShapeDtypeStruct((8, PAD), jnp.int32),
                   jax.ShapeDtypeStruct((PAD, 8 * B), F32)],
        cost_estimate=pl.CostEstimate(flops=10_000_000, bytes_accessed=300_000, transcendentals=0),
        name="route",
    )(ids, a_cols_t, *cols, sel)


def load_pool(parts, pool_ref, sems):
    copies = []
    start = 0
    for n, part in enumerate(parts):
        copies.append(pltpu.make_async_copy(part, pool_ref.at[pl.ds(start, part.shape[0])], sems.at[n]))
        start += part.shape[0]
    for copy in copies:
        copy.start()
    for copy in copies:
        copy.wait()


def merge_row(i, place, row, src_ref, mask_ref, a_ref, pool_ref, merged_ref):
    index = [src_ref[k, row] for k in range(7)]
    w = jnp.concatenate([pool_ref[j] for j in index] + [pool_ref[index[0]]], axis=0)
    a = a_ref[i]
    mask = jnp.broadcast_to(mask_ref[pl.ds(row, 1), :], a.shape).astype(BF16)
    a_own = a * mask
    both = jnp.concatenate([a_own, a - a_own], axis=0)
    merged = jnp.dot(both, w, preferred_element_type=F32).astype(BF16)
    if isinstance(place, int):
        rows = slice(place * B, place * B + B)
    else:
        rows = pl.ds(pl.multiple_of(place * B, B), B)
    merged_ref[rows, :4 * B] = merged[:B]
    merged_ref[rows, 4 * B:] = merged[B:]


def tn(x, y):
    return lax.dot_general(x, y, (((0,), (0,)), ((), ())), preferred_element_type=F32)


def straddle_kernel(src_ref, mask_ref, a_ref, *refs):
    parts, (out_ref, pool_ref, merged_ref, sems) = refs[:5], refs[5:]
    load_pool(parts, pool_ref, sems)
    for i in range(HALF):
        merge_row(i, i, HALF + i, src_ref, mask_ref, a_ref, pool_ref, merged_ref)
    own = pool_ref[HALF:FS].reshape(HALF * B, KG * B)
    out_ref[...] = tn(own, merged_ref[...]).astype(BF16)


def straddle(src, mask, a_rows, parts):
    anywhere = pl.BlockSpec(memory_space=pl.ANY)
    return pl.pallas_call(
        straddle_kernel,
        grid=(1,),
        in_specs=[
            pl.BlockSpec(memory_space=pltpu.SMEM),
            pl.BlockSpec((PAD, 8 * B), lambda g: (0, 0)),
            pl.BlockSpec((HALF, B, 8 * B), lambda g: (1, 0, 0)),
        ] + [anywhere] * 5,
        out_specs=pl.BlockSpec((KG * B, 8 * B), lambda g: (0, 0)),
        out_shape=jax.ShapeDtypeStruct((KG * B, 8 * B), BF16),
        scratch_shapes=[
            pltpu.VMEM((POOL, B, KG * B), BF16),
            pltpu.VMEM((HALF * B, 8 * B), BF16),
            pltpu.SemaphoreType.DMA((5,)),
        ],
        compiler_params=pltpu.CompilerParams(vmem_limit_bytes=VMEM_BYTES),
        cost_estimate=pl.CostEstimate(flops=300_000_000, bytes_accessed=6_000_000, transcendentals=0),
        name="straddle",
    )(src, mask, a_rows, *parts)


def order_slots(c_cols_ref, set_id, first_row, place_ref):
    for r in range(KG):
        for s in range(8):
            c = c_cols_ref[s, first_row + r]
            u = (c & 3) + jnp.where((c >> 2) == set_id, 0, 4)
            place_ref[r, u] = s


def store_blocks(total, place_ref, out_ref):
    for r in range(KG):
        for u in range(8):
            block = total[r * B:(r + 1) * B, u * B:(u + 1) * B]
            out_ref[r, place_ref[r, u]] = block.astype(BF16)


def sets_kernel(base_ref, src_ref, c_cols_ref, mask_ref, a_ref, *refs):
    parts, (out_ref, first_ref, pool_ref, merged_ref, place_ref, sems) = refs[:5], refs[5:]
    s = pl.program_id(0)

    @pl.when(s == 0)
    def _():
        load_pool(parts, pool_ref, sems)
        merged_ref[HALF * B:, :] = jnp.zeros((HALF * B, 8 * B), BF16)

    for i in range(HALF):
        merge_row(i, i, s * FS + i, src_ref, mask_ref, a_ref, pool_ref, merged_ref)

    @pl.when(s > 0)
    def _():
        for i in range(HALF, FS):
            merge_row(i, i, s * FS + i, src_ref, mask_ref, a_ref, pool_ref, merged_ref)

    own = pool_ref[pl.ds(s * FS, FS)].reshape(FS * B, KG * B)
    total = tn(own, merged_ref[...])

    @pl.when(s == 0)
    def _():
        first_ref[...] = total

    order_slots(c_cols_ref, base_ref[0] + s, s * KG, place_ref)
    store_blocks(total, place_ref, out_ref)


def sets(base, src, c_cols_t, mask, a_rows, parts):
    anywhere = pl.BlockSpec(memory_space=pl.ANY)
    smem = pl.BlockSpec(memory_space=pltpu.SMEM)
    return pl.pallas_call(
        sets_kernel,
        grid=(SETS,),
        in_specs=[
            smem, smem, smem,
            pl.BlockSpec((PAD, 8 * B), lambda s: (0, 0)),
            pl.BlockSpec((FS, B, 8 * B), lambda s: (s, 0, 0)),
        ] + [anywhere] * 5,
        out_specs=[
            pl.BlockSpec((KG, 8, B, B), lambda s: (s, 0, 0, 0)),
            pl.BlockSpec((KG * B, 8 * B), lambda s: (0, 0)),
        ],
        out_shape=[
            jax.ShapeDtypeStruct((SETS * KG, 8, B, B), BF16),
            jax.ShapeDtypeStruct((KG * B, 8 * B), F32),
        ],
        scratch_shapes=[
            pltpu.VMEM((POOL, B, KG * B), BF16),
            pltpu.VMEM((FS * B, 8 * B), BF16),
            pltpu.SMEM((KG, 8), jnp.int32),
            pltpu.SemaphoreType.DMA((5,)),
        ],
        compiler_params=pltpu.CompilerParams(vmem_limit_bytes=VMEM_BYTES),
        cost_estimate=pl.CostEstimate(flops=4_000_000_000, bytes_accessed=14_000_000, transcendentals=0),
        name="sets",
    )(base, src, c_cols_t, mask, a_rows, *parts)


def finish_kernel(base_ref, c_cols_ref, first_ref, incoming_ref, whole_ref, out_ref, place_ref):
    order_slots(c_cols_ref, base_ref[0], 0, place_ref)
    store_blocks(first_ref[...] + incoming_ref[...].astype(F32), place_ref, out_ref)


def finish(base, c_cols_t, first, incoming, whole):
    smem = pl.BlockSpec(memory_space=pltpu.SMEM)
    return pl.pallas_call(
        finish_kernel,
        grid=(1,),
        in_specs=[
            smem, smem,
            pl.BlockSpec((KG * B, 8 * B), lambda g: (0, 0)),
            pl.BlockSpec((KG * B, 8 * B), lambda g: (0, 0)),
            pl.BlockSpec(memory_space=pl.ANY),
        ],
        out_specs=pl.BlockSpec((KG, 8, B, B), lambda g: (0, 0, 0, 0)),
        out_shape=jax.ShapeDtypeStruct((SETS * KG, 8, B, B), BF16),
        scratch_shapes=[pltpu.SMEM((KG, 8), jnp.int32)],
        input_output_aliases={4: 0},
        compiler_params=pltpu.CompilerParams(vmem_limit_bytes=VMEM_BYTES),
        name="finish",
    )(base, c_cols_t, first, incoming, whole)


def shards(a_blocks, a_cols, p_blocks, p_cols, c_cols):
    dom_count = lax.axis_size("dom")
    sub_count = lax.axis_size("sub")
    dom = lax.axis_index("dom")
    sub = lax.axis_index("sub")
    device = dom * sub_count + sub
    ids = jnp.stack([
        device,
        (dom + dom_count - 1) % dom_count * sub_count + sub,
        (dom + 1) % dom_count * sub_count + sub,
        dom * sub_count + (sub + sub_count - 1) % sub_count,
        dom * sub_count + (sub + 1) % sub_count,
    ]).astype(jnp.int32)
    base = ids[:1] * SETS
    cols_t = p_cols.T
    moves = (("dom", 1), ("dom", -1), ("sub", 1), ("sub", -1))
    cols = [cols_t] + [passed_along(cols_t, axis, step) for axis, step in moves]
    pool, up, down, fore, back, sel = prolong(base, cols_t, p_blocks.transpose(1, 2, 3, 0))
    parts = [pool] + [
        passed_along(rows, axis, step) for rows, (axis, step) in zip((up, down, fore, back), moves)
    ]
    a_rows = operator(sel, a_blocks.transpose(1, 2, 3, 0))
    src, mask = route(ids, a_cols.T, cols, sel)
    partial = straddle(src, mask, a_rows, parts)
    incoming = passed_along(partial, "sub", 1)
    whole, first = sets(base, src, c_cols.T, mask, a_rows, parts)
    return finish(base, c_cols.T, first, incoming, whole)


def solution(mesh):
    spec4 = P(("dom", "sub"), None, None, None)
    spec2 = P(("dom", "sub"), None)
    return jax.shard_map(
        shards, mesh=mesh, in_specs=(spec4, spec2, spec4, spec2, spec2), out_specs=spec4,
        check_vma=False,
    )
```

```python
import jax
import jax.numpy as jnp
from jax import lax
from jax.experimental import pallas as pl
from jax.experimental.pallas import tpu as pltpu
from jax.sharding import PartitionSpec as P

KG = 4
FS = 14
HALF = FS // 2
ROWS = 84
PAD = 88
SETS = 6
B = 64
POOL = ROWS + FS + FS + HALF + HALF + FS
F32 = jnp.float32
BF16 = jnp.bfloat16
VMEM_BYTES = 56 * 1024 * 1024


def passed_along(block, axis, distance):
    n = lax.axis_size(axis)
    return lax.ppermute(block, axis, [((i - distance) % n, i) for i in range(n)])


def iota(shape, dim):
    return lax.broadcasted_iota(jnp.int32, shape, dim)


QUARTERS = 4
CHUNK = B // QUARTERS
STRIDE = 89
SENDS = (((70, 14),), ((56, 14),), ((7, 7),), ((0, 7), (14, 14)))
ANY = pl.BlockSpec(memory_space=pl.ANY)
SMEM = pl.BlockSpec(memory_space=pltpu.SMEM)
VMEM = pl.BlockSpec(memory_space=pltpu.VMEM)


def call(kernel, name, ins, outs, scratch, flops, nbytes, aliases=None):
    return pl.pallas_call(
        kernel,
        in_specs=ins,
        out_specs=[spec for spec, _ in outs],
        out_shape=[jax.ShapeDtypeStruct(*shape) for _, shape in outs],
        scratch_shapes=scratch,
        input_output_aliases=aliases or {},
        compiler_params=pltpu.CompilerParams(vmem_limit_bytes=VMEM_BYTES),
        cost_estimate=pl.CostEstimate(flops=flops, bytes_accessed=nbytes, transcendentals=0),
        name=name,
    )


def groups(lead, set_base):
    group = (lead >> 2) - set_base
    own = (group >= 0) & (group < SETS)
    return jnp.where(own, jnp.where(group > 0, group + 1, 0), 1)


def to_column(row):
    wide = jnp.broadcast_to(row, (ROWS, ROWS))
    diagonal = iota((ROWS, ROWS), 0) == iota((ROWS, ROWS), 1)
    return jnp.sum(jnp.where(diagonal, wide, 0.0), axis=1, keepdims=True)


def ranks(key):
    order = (key * 128 + iota((1, ROWS), 1)).astype(F32)
    return jnp.sum(jnp.where(to_column(order) < order, 1.0, 0.0), axis=0, keepdims=True)


def nt(x, y):
    return lax.dot_general(x, y, (((1,), (1,)), ((), ())), preferred_element_type=F32)


def tn(x, y):
    return lax.dot_general(x, y, (((0,), (0,)), ((), ())), preferred_element_type=F32)


def quarter(c):
    return pl.ds(pl.multiple_of(c * CHUNK, CHUNK), CHUNK)


def send_copies(c, pool_ref, send_refs, sems):
    copies = []
    for ref, runs in zip(send_refs, SENDS):
        total = sum(n for _, n in runs)
        done = 0
        for first, n in runs:
            copies.append(pltpu.make_async_copy(
                pool_ref.at[pl.ds(first, n), quarter(c)],
                ref.at[pl.ds(c * total + done, n)],
                sems.at[c, len(copies)],
            ))
            done += n
    return copies


def prolong_kernel(base_ref, cols_ref, p_hbm, pool_hbm, up_hbm, down_hbm, fore_hbm, back_hbm,
                   sel_ref, order_ref, p_ref, pool_ref, ids_ref, t0_ref, t1_ref,
                   in_sems, out_sems, id_sems):
    def fetch(c):
        return pltpu.make_async_copy(p_hbm.at[:, quarter(c)], p_ref.at[:, quarter(c)], in_sems.at[c])

    sends = (up_hbm, down_hbm, fore_hbm, back_hbm)

    def stores(c):
        whole = pltpu.make_async_copy(
            pool_ref.at[:, quarter(c)], pool_hbm.at[:, quarter(c)], out_sems.at[c, 5])
        return send_copies(c, pool_ref, sends, out_sems) + [whole]

    for c in range(QUARTERS):
        fetch(c).start()
    rank = ranks(groups(cols_ref[0:1, :], base_ref[0]))
    sel = jnp.where(rank.astype(jnp.int32) == iota((PAD, ROWS), 0), 1.0, 0.0).astype(BF16)
    sel_ref[...] = sel
    order = nt(iota((16, ROWS), 1).astype(F32).astype(BF16), sel)
    order_ref[...] = order[:8].astype(jnp.int32)
    ids_ref[...] = jnp.zeros((16, KG * B), BF16)
    ids_ref[:, :PAD] = order.astype(BF16)
    id_copies = []
    for n, ref in enumerate(sends):
        id_copies.append(pltpu.make_async_copy(ids_ref, ref.at[ref.shape[0] - 1], id_sems.at[n]))
    for copy in id_copies:
        copy.start()
    place = cols_ref[...] & 3
    weights = [
        [jnp.where(place[q:q + 1, :] == r, 1.0, 0.0).astype(BF16) for q in range(3)]
        for r in range(KG)
    ]

    def step(c, carry):
        fetch(c).wait()
        for b in range(CHUNK):
            x = [p_ref[q, c * CHUNK + b] for q in range(3)]
            y = [x[0] * w[0] + x[1] * w[1] + x[2] * w[2] for w in weights]
            t = nt(sel, jnp.concatenate(y, axis=0))
            t0_ref[b * STRIDE:b * STRIDE + PAD, :] = t[:, :128]
            t1_ref[b * STRIDE:b * STRIDE + PAD, :] = t[:, 128:]
        for i in range(ROWS):
            pool_ref[i, quarter(c), :] = jnp.concatenate(
                [t[pl.ds(i, CHUNK, stride=STRIDE), :] for t in (t0_ref, t1_ref)], axis=1
            ).astype(BF16)
        for copy in stores(c):
            copy.start()
        return carry

    lax.fori_loop(0, QUARTERS, step, 0)
    for copy in id_copies:
        copy.wait()
    for c in range(QUARTERS):
        for copy in stores(c):
            copy.wait()


def prolong(base, cols_t, p_t):
    def rows(n):
        return ANY, ((QUARTERS * n + 1, CHUNK, KG * B), BF16)

    return call(
        prolong_kernel, "prolong", [SMEM, VMEM, ANY],
        [(ANY, ((ROWS, B, KG * B), BF16)), rows(14), rows(14), rows(7), rows(21),
         (VMEM, ((PAD, ROWS), BF16)), (VMEM, ((8, PAD), jnp.int32))],
        [
            pltpu.VMEM((3, B, B, ROWS), BF16),
            pltpu.VMEM((ROWS, B, KG * B), BF16),
            pltpu.VMEM((16, KG * B), BF16),
            pltpu.VMEM((CHUNK * STRIDE, 128), F32),
            pltpu.VMEM((CHUNK * STRIDE, 128), F32),
            pltpu.SemaphoreType.DMA((QUARTERS,)),
            pltpu.SemaphoreType.DMA((QUARTERS, 6)),
            pltpu.SemaphoreType.DMA((4,)),
        ],
        400_000_000, 8_000_000,
    )(base, cols_t, p_t)


def set_name(slot):
    name = jnp.where(slot < 7, 0.0, 1.0)
    for start, value in ((14, 2.0), (28, 3.0), (42, 4.0), (56, 5.0), (70, 6.0), (84, 7.0),
                         (98, 8.0), (112, 0.0), (119, 1.0), (126, 9.0)):
        name = jnp.where(slot >= start, value, name)
    return name


def own_mask(src, key, sel):
    own = jnp.where(set_name(src) == key, 1.0, 0.0)
    by_row = nt(sel, own.astype(BF16)).astype(BF16)
    spread = jnp.where(iota((8, 8 * B), 1) >> 6 == iota((8, 8 * B), 0), 1.0, 0.0).astype(BF16)
    return jnp.dot(by_row, spread, preferred_element_type=F32)


def sorted_slots(src, sel):
    return nt(jnp.maximum(src, 0.0).astype(BF16), sel).astype(jnp.int32)


def merge_row(i, place, row, src_ref, mask_ref, a_ref, pool_ref, merged_ref):
    index = [src_ref[k, row] for k in range(7)]
    w = jnp.concatenate([pool_ref[j] for j in index] + [pool_ref[index[0]]], axis=0)
    a = a_ref[i]
    mask = jnp.broadcast_to(mask_ref[pl.ds(row, 1), :], a.shape).astype(BF16)
    a_own = a * mask
    both = jnp.concatenate([a_own, a - a_own], axis=0)
    merged = jnp.dot(both, w, preferred_element_type=F32).astype(BF16)
    merged_ref[place * B:place * B + B, :KG * B] = merged[:B]
    merged_ref[place * B:place * B + B, KG * B:] = merged[B:]


def order_slots(c_cols_ref, set_id, first_row, place_ref):
    for r in range(KG):
        for s in range(8):
            c = c_cols_ref[s, first_row + r]
            u = (c & 3) + jnp.where((c >> 2) == set_id, 0, 4)
            place_ref[r, u] = s


def store_blocks(total, first_row, place_ref, out_ref):
    total = total.astype(BF16)
    for r in range(KG):
        for u in range(8):
            out_ref[first_row + r, place_ref[r, u]] = total[r * B:(r + 1) * B, u * B:(u + 1) * B]


def one_set(s, set_base, src_ref, c_cols_ref, mask_ref, a_ref, pool_ref, merged_ref, place_ref,
            blocks_ref):
    first = s * FS
    order_slots(c_cols_ref, set_base + s, s * KG, place_ref)
    for i in range(FS):
        merge_row(first + i, i, first + i, src_ref, mask_ref, a_ref, pool_ref, merged_ref)
    own = pool_ref[pl.ds(first, FS)].reshape(FS * B, KG * B)
    store_blocks(tn(own, merged_ref[...]), s * KG, place_ref, blocks_ref)


def operator_kernel(base_ref, order_ref, c_cols_ref, cols_ref, a_cols_ref, sel_ref, a_hbm, pool_hbm,
                    a_rows_hbm, out_hbm, local_ref, flags_ref,
                    a_ref, rows_ref, pool_ref, blocks_ref, merged_ref, mask_ref, src_v, src_ref,
                    flag_s, place_ref, t0, t1, t2, t3, in_sems, sems, out_sems):
    def fetch(c):
        return pltpu.make_async_copy(a_hbm.at[:, quarter(c)], a_ref.at[:, quarter(c)], in_sems.at[c])

    for c in range(QUARTERS):
        fetch(c).start()
    load = pltpu.make_async_copy(pool_hbm, pool_ref, sems.at[0])
    load.start()

    key = groups(cols_ref[0:1, :], base_ref[0])
    rank = to_column(ranks(key)) + 1.0
    row = iota((ROWS, ROWS), 0)
    first_row = base_ref[0] // SETS * ROWS
    sources = [
        jnp.sum(jnp.where(a_cols_ref[k:k + 1, :] - first_row == row, rank, 0.0), axis=0,
                keepdims=True) - 1.0
        for k in range(7)
    ]
    src = jnp.concatenate(sources + [sources[0]], axis=0)
    keys = key.astype(F32)
    local_ref[...] = jnp.where(iota((8, ROWS), 0) < 7, src, keys)
    away = jnp.max(jnp.where(src < 0.0, 1.0, 0.0), axis=0, keepdims=True)
    away = jnp.sum(jnp.where(iota((8, ROWS), 0).astype(F32) == keys, away, 0.0), axis=1, keepdims=True)
    flags_ref[...] = jnp.broadcast_to(away, (8, 128)).astype(jnp.int32)
    sel = sel_ref[...]
    src_v[:, :PAD] = sorted_slots(src, sel)
    src_v[:, PAD:] = jnp.zeros((8, 128 - PAD), jnp.int32)
    mask_ref[...] = own_mask(src, keys, sel)
    to_smem = [pltpu.make_async_copy(src_v, src_ref, sems.at[1]),
               pltpu.make_async_copy(flags_ref, flag_s, sems.at[2])]
    for copy in to_smem:
        copy.start()

    t_refs = (t0, t1, t2, t3)

    def step(c, carry):
        fetch(c).wait()
        for a in range(CHUNK):
            zero = jnp.zeros((B, ROWS), BF16)
            x = [a_ref[k, c * CHUNK + a] for k in range(7)] + [zero]
            for h in range(4):
                pair = jnp.concatenate(x[2 * h:2 * h + 2], axis=0)
                t_refs[h][a * STRIDE:a * STRIDE + ROWS, :] = jnp.transpose(pair).astype(F32)
        for i in range(ROWS):
            rows_ref[i, quarter(c), :] = jnp.concatenate(
                [t[pl.ds(order_ref[0, i], CHUNK, stride=STRIDE), :] for t in t_refs], axis=1
            ).astype(BF16)
        return carry

    lax.fori_loop(0, QUARTERS, step, 0)
    keep = pltpu.make_async_copy(rows_ref, a_rows_hbm, sems.at[3])
    keep.start()
    load.wait()
    for copy in to_smem:
        copy.wait()

    def store(s):
        rows = pl.ds(s * KG, KG)
        return pltpu.make_async_copy(blocks_ref.at[rows], out_hbm.at[rows], out_sems.at[s])

    def work(s, carry):
        @pl.when(flag_s[s + 1, 0] == 0)
        def _():
            one_set(s, base_ref[0], src_ref, c_cols_ref, mask_ref, rows_ref, pool_ref, merged_ref,
                    place_ref, blocks_ref)
            store(s).start()
        return carry

    lax.fori_loop(1, SETS, work, 0)

    def end(s, carry):
        @pl.when(flag_s[s + 1, 0] == 0)
        def _():
            store(s).wait()
        return carry

    lax.fori_loop(1, SETS, end, 0)
    keep.wait()


def operator(base, order, c_cols_t, cols_t, a_cols_t, sel, a_t, pool):
    return call(
        operator_kernel, "operator", [SMEM, SMEM, SMEM, VMEM, VMEM, VMEM, ANY, ANY],
        [(ANY, ((ROWS, B, 8 * B), BF16)), (ANY, ((SETS * KG, 8, B, B), BF16)),
         (VMEM, ((8, ROWS), F32)), (VMEM, ((8, 128), jnp.int32))],
        [
            pltpu.VMEM((7, B, B, ROWS), BF16),
            pltpu.VMEM((ROWS, B, 8 * B), BF16),
            pltpu.VMEM((ROWS, B, KG * B), BF16),
            pltpu.VMEM((SETS * KG, 8, B, B), BF16),
            pltpu.VMEM((FS * B, 8 * B), BF16),
            pltpu.VMEM((PAD, 8 * B), F32),
            pltpu.VMEM((8, 128), jnp.int32),
            pltpu.SMEM((8, 128), jnp.int32),
            pltpu.SMEM((8, 128), jnp.int32),
            pltpu.SMEM((KG, 8), jnp.int32),
        ] + [pltpu.VMEM((CHUNK * STRIDE, 128), F32)] * 4 + [
            pltpu.SemaphoreType.DMA((QUARTERS,)),
            pltpu.SemaphoreType.DMA((4,)),
            pltpu.SemaphoreType.DMA((SETS,)),
        ],
        4_000_000_000, 18_000_000,
    )(base, order, c_cols_t, cols_t, a_cols_t, sel, a_t, pool)


def pool_copies(parts, pool_ref, sems):
    copies = [pltpu.make_async_copy(parts[0], pool_ref.at[pl.ds(0, ROWS)], sems.at[0, 0])]
    start = ROWS
    for n, part in enumerate(parts[1:]):
        rows = (part.shape[0] - 1) // QUARTERS
        for c in range(QUARTERS):
            copies.append(pltpu.make_async_copy(
                part.at[pl.ds(c * rows, rows)],
                pool_ref.at[pl.ds(start, rows), pl.ds(c * CHUNK, CHUNK)],
                sems.at[n + 1, c],
            ))
        start += rows
    return copies


def straddle_kernel(ids_ref, a_cols_ref, local_ref, sel_ref, a_rows_hbm, *refs):
    parts = refs[:5]
    (out_ref, src_out, mask_ref, pool_ref, rows_ref, names_ref, merged_ref, src_ref, sems,
     name_sems, extra_sems) = refs[5:]
    names = [
        pltpu.make_async_copy(part.at[part.shape[0] - 1], names_ref.at[n], name_sems.at[n])
        for n, part in enumerate(parts[1:])
    ]
    for copy in names:
        copy.start()
    loads = pool_copies(parts, pool_ref, sems)
    loads.append(pltpu.make_async_copy(a_rows_hbm.at[pl.ds(HALF, HALF)], rows_ref, extra_sems.at[0]))
    for copy in loads:
        copy.start()
    for copy in names:
        copy.wait()
    shifts = (((70, 84, 84 - 70),), ((56, 70, 98 - 56),), ((7, 14, 112 - 7),),
              ((0, 7, 119), (14, 28, 126 - 14)))
    near = ((64, 88), (56, 72), (0, 16), (0, 32))
    found = [jnp.zeros((1, ROWS), F32)] * 7
    for n in range(4):
        low, high = near[n]
        column = jnp.transpose(names_ref[n][:, :128].astype(F32))[low:high, 0:1].astype(jnp.int32)
        row = iota((high - low, 1), 0) + low
        slot = jnp.zeros((high - low, 1), jnp.int32)
        for first, last, shift in shifts[n]:
            slot = jnp.where((row >= first) & (row < last), row + shift + 1, slot)
        column = jnp.where(slot > 0, column + ids_ref[n + 1] * ROWS, -1)
        slot = slot.astype(F32)
        for k in range(7):
            found[k] = found[k] + jnp.sum(
                jnp.where(a_cols_ref[k:k + 1, :] == column, slot, 0.0), axis=0, keepdims=True)
    local = local_ref[...]
    away = jnp.concatenate(found + [found[0]], axis=0) - 1.0
    src = jnp.where(local >= 0.0, local, away)
    src = jnp.where(iota((8, ROWS), 0) < 7, src, jnp.broadcast_to(src[0:1, :], (8, ROWS)))
    sel = sel_ref[...]
    src_out[:, :PAD] = sorted_slots(src, sel)
    src_out[:, PAD:] = jnp.zeros((8, 128 - PAD), jnp.int32)
    to_smem = pltpu.make_async_copy(src_out, src_ref, extra_sems.at[1])
    to_smem.start()
    mask_ref[...] = own_mask(src, local[7:8, :], sel)
    to_smem.wait()
    for copy in loads:
        copy.wait()
    for i in range(HALF):
        merge_row(i, i, HALF + i, src_ref, mask_ref, rows_ref, pool_ref, merged_ref)
    own = pool_ref[HALF:FS].reshape(HALF * B, KG * B)
    out_ref[...] = tn(own, merged_ref[...]).astype(BF16)


def straddle(ids, a_cols_t, local, sel, a_rows, parts):
    return call(
        straddle_kernel, "straddle", [SMEM, VMEM, VMEM, VMEM, ANY] + [ANY] * 5,
        [(VMEM, ((KG * B, 8 * B), BF16)), (VMEM, ((8, 128), jnp.int32)), (VMEM, ((PAD, 8 * B), F32))],
        [
            pltpu.VMEM((POOL, B, KG * B), BF16),
            pltpu.VMEM((HALF, B, 8 * B), BF16),
            pltpu.VMEM((4, 16, KG * B), BF16),
            pltpu.VMEM((HALF * B, 8 * B), BF16),
            pltpu.SMEM((8, 128), jnp.int32),
            pltpu.SemaphoreType.DMA((5, QUARTERS)),
            pltpu.SemaphoreType.DMA((4,)),
            pltpu.SemaphoreType.DMA((2,)),
        ],
        300_000_000, 6_000_000,
    )(ids, a_cols_t, local, sel, a_rows, *parts)


def sets_kernel(base_ref, src_ref, flag_ref, c_cols_ref, mask_ref, a_rows_hbm, *refs):
    parts = refs[:5]
    (_, out_hbm, first_ref, pool_ref, rows_ref, blocks_ref, merged_ref, place_ref, sems, row_sems,
     out_sems) = refs[5:]
    loads = pool_copies(parts, pool_ref, sems)

    def fetch(s):
        rows = pl.ds(s * FS, FS)
        return pltpu.make_async_copy(a_rows_hbm.at[rows], rows_ref.at[rows], row_sems.at[s])

    def store(s):
        rows = pl.ds(s * KG, KG)
        return pltpu.make_async_copy(blocks_ref.at[rows], out_hbm.at[rows], out_sems.at[s])

    def here(s):
        return flag_ref[s + 1, 0] != 0

    fetch(0).start()
    for copy in loads:
        copy.start()
    for s in range(1, SETS):
        @pl.when(here(s))
        def _(s=s):
            fetch(s).start()
    fetch(0).wait()
    for copy in loads:
        copy.wait()
    for i in range(HALF):
        merge_row(i, i, i, src_ref, mask_ref, rows_ref, pool_ref, merged_ref)
    own = pool_ref[:HALF].reshape(HALF * B, KG * B)
    first_ref[...] = tn(own, merged_ref[:HALF * B, :])

    def work(s, carry):
        @pl.when(here(s))
        def _():
            fetch(s).wait()
            one_set(s, base_ref[0], src_ref, c_cols_ref, mask_ref, rows_ref, pool_ref, merged_ref,
                    place_ref, blocks_ref)
            store(s).start()
        return carry

    lax.fori_loop(1, SETS, work, 0)

    def end(s, carry):
        @pl.when(here(s))
        def _():
            store(s).wait()
        return carry

    lax.fori_loop(1, SETS, end, 0)


def sets(base, src, flags, c_cols_t, mask, a_rows, parts, whole):
    return call(
        sets_kernel, "sets", [SMEM, SMEM, SMEM, SMEM, VMEM, ANY] + [ANY] * 6,
        [(ANY, ((SETS * KG, 8, B, B), BF16)), (VMEM, ((KG * B, 8 * B), F32))],
        [
            pltpu.VMEM((POOL, B, KG * B), BF16),
            pltpu.VMEM((ROWS, B, 8 * B), BF16),
            pltpu.VMEM((SETS * KG, 8, B, B), BF16),
            pltpu.VMEM((FS * B, 8 * B), BF16),
            pltpu.SMEM((KG, 8), jnp.int32),
            pltpu.SemaphoreType.DMA((5, QUARTERS)),
            pltpu.SemaphoreType.DMA((SETS,)),
            pltpu.SemaphoreType.DMA((SETS,)),
        ],
        2_500_000_000, 12_000_000, aliases={11: 0},
    )(base, src, flags, c_cols_t, mask, a_rows, *parts, whole)


def finish_kernel(base_ref, c_cols_ref, first_ref, incoming_ref, _, out_hbm, blocks_ref, place_ref,
                  sem):
    order_slots(c_cols_ref, base_ref[0], 0, place_ref)
    store_blocks(first_ref[...] + incoming_ref[...].astype(F32), 0, place_ref, blocks_ref)
    copy = pltpu.make_async_copy(blocks_ref, out_hbm.at[pl.ds(0, KG)], sem)
    copy.start()
    copy.wait()


def finish(base, c_cols_t, first, incoming, whole):
    return call(
        finish_kernel, "finish", [SMEM, SMEM, VMEM, VMEM, ANY],
        [(ANY, ((SETS * KG, 8, B, B), BF16))],
        [pltpu.VMEM((KG, 8, B, B), BF16), pltpu.SMEM((KG, 8), jnp.int32), pltpu.SemaphoreType.DMA],
        1_000_000, 1_500_000, aliases={4: 0},
    )(base, c_cols_t, first, incoming, whole)[0]


def shards(a_blocks, a_cols, p_blocks, p_cols, c_cols):
    dom_count = lax.axis_size("dom")
    sub_count = lax.axis_size("sub")
    dom = lax.axis_index("dom")
    sub = lax.axis_index("sub")
    device = dom * sub_count + sub
    ids = jnp.stack([
        device,
        (dom + dom_count - 1) % dom_count * sub_count + sub,
        (dom + 1) % dom_count * sub_count + sub,
        dom * sub_count + (sub + sub_count - 1) % sub_count,
        dom * sub_count + (sub + 1) % sub_count,
    ]).astype(jnp.int32)
    base = ids[:1] * SETS
    cols_t, a_cols_t, c_cols_t = p_cols.T, a_cols.T, c_cols.T
    moves = (("dom", 1), ("dom", -1), ("sub", 1), ("sub", -1))
    pool, *sends, sel, order = prolong(base, cols_t, p_blocks.transpose(1, 2, 3, 0))
    parts = [pool] + [passed_along(rows, axis, step) for rows, (axis, step) in zip(sends, moves)]
    a_rows, whole, local, flags = operator(
        base, order, c_cols_t, cols_t, a_cols_t, sel, a_blocks.transpose(1, 2, 3, 0), pool)
    partial, src, mask = straddle(ids, a_cols_t, local, sel, a_rows, parts)
    incoming = passed_along(partial, "sub", 1)
    whole, first = sets(base, src, flags, c_cols_t, mask, a_rows, parts, whole)
    return finish(base, c_cols_t, first, incoming, whole)


def solution(mesh):
    spec4 = P(("dom", "sub"), None, None, None)
    spec2 = P(("dom", "sub"), None)
    return jax.shard_map(
        shards, mesh=mesh, in_specs=(spec4, spec2, spec4, spec2, spec2), out_specs=spec4,
        check_vma=False,
    )
```

```python
import jax
import jax.numpy as jnp
from jax import lax
from jax.experimental import pallas as pl
from jax.experimental.pallas import tpu as pltpu
from jax.sharding import PartitionSpec as P

KG = 4
FS = 14
HALF = FS // 2
ROWS = 84
PAD = 88
SETS = 6
B = 64
POOL = ROWS + FS + FS + HALF + HALF + FS
F32 = jnp.float32
BF16 = jnp.bfloat16


def passed_along(block, axis, distance):
    n = lax.axis_size(axis)
    return lax.ppermute(block, axis, [((i - distance) % n, i) for i in range(n)])


def iota(shape, dim):
    return lax.broadcasted_iota(jnp.int32, shape, dim)


QUARTERS = 4
CHUNK = B // QUARTERS
STRIDE = 89
SENDS = (((70, 14),), ((56, 14),), ((7, 7),), ((0, 7), (14, 14)))
ANY = pl.BlockSpec(memory_space=pl.ANY)
HBM = pl.BlockSpec(memory_space=pltpu.HBM)


def call(kernel, name, ins, outs, scratch, flops, nbytes, vmem, aliases=None, grid=()):
    return pl.pallas_call(
        kernel,
        grid=grid,
        in_specs=ins,
        out_specs=[ANY] * len(outs),
        out_shape=[jax.ShapeDtypeStruct(*shape) for shape in outs],
        scratch_shapes=scratch,
        input_output_aliases=aliases or {},
        compiler_params=pltpu.CompilerParams(vmem_limit_bytes=vmem * 1024 * 1024),
        cost_estimate=pl.CostEstimate(flops=flops, bytes_accessed=nbytes, transcendentals=0),
        name=name,
    )


def devices():
    dom_count, sub_count = lax.axis_size("dom"), lax.axis_size("sub")
    dom, sub = lax.axis_index("dom"), lax.axis_index("sub")

    def number(d, s):
        return lax.rem(d, dom_count) * sub_count + lax.rem(s, sub_count)

    return [number(dom, sub), number(dom + dom_count - 1, sub), number(dom + 1, sub),
            number(dom, sub + sub_count - 1), number(dom, sub + 1)]


def begin(copies):
    for copy in copies:
        copy.start()


def finished(copies):
    for copy in copies:
        copy.wait()


def load_all(pairs, sems):
    return [pltpu.make_async_copy(src, dst, sems.at[n]) for n, (src, dst) in enumerate(pairs)]


def groups(lead, set_base):
    group = (lead >> 2) - set_base
    own = (group >= 0) & (group < SETS)
    return jnp.where(own, jnp.where(group > 0, group + 1, 0), 1)


def to_column(row):
    wide = jnp.broadcast_to(row, (ROWS, ROWS))
    diagonal = iota((ROWS, ROWS), 0) == iota((ROWS, ROWS), 1)
    return jnp.sum(jnp.where(diagonal, wide, 0.0), axis=1, keepdims=True)


def ranks(key):
    order = (key * 128 + iota((1, ROWS), 1)).astype(F32)
    return jnp.sum(jnp.where(to_column(order) < order, 1.0, 0.0), axis=0, keepdims=True)


def selector(rank):
    return jnp.where(rank.astype(jnp.int32) == iota((PAD, ROWS), 0), 1.0, 0.0).astype(BF16)


def sorted_order(sel):
    return nt(iota((16, ROWS), 1).astype(F32).astype(BF16), sel)


def nt(x, y):
    return lax.dot_general(x, y, (((1,), (1,)), ((), ())), preferred_element_type=F32)


def tn(x, y):
    return lax.dot_general(x, y, (((0,), (0,)), ((), ())), preferred_element_type=F32)


def quarter(c):
    return pl.ds(pl.multiple_of(c * CHUNK, CHUNK), CHUNK)


def send_copies(c, pool_ref, send_refs, sems):
    copies = []
    for ref, runs in zip(send_refs, SENDS):
        total = sum(n for _, n in runs)
        done = 0
        for first, n in runs:
            copies.append(pltpu.make_async_copy(
                pool_ref.at[pl.ds(first, n), quarter(c)],
                ref.at[pl.ds(c * total + done, n)],
                sems.at[c, len(copies)],
            ))
            done += n
    return copies


def prolong_kernel(cols_ref, p_ref, pool_hbm, up_hbm, down_hbm, fore_hbm, back_hbm,
                   sel_ref, pool_ref, ids_ref, t0_ref, t1_ref, out_sems, id_sems):
    c = pl.program_id(0)
    sends = (up_hbm, down_hbm, fore_hbm, back_hbm)

    def stores(c):
        whole = pltpu.make_async_copy(
            pool_ref.at[:, quarter(c)], pool_hbm.at[:, quarter(c)], out_sems.at[c, 5])
        return send_copies(c, pool_ref, sends, out_sems) + [whole]

    id_copies = [pltpu.make_async_copy(ids_ref, ref.at[ref.shape[0] - 1], id_sems.at[n])
                 for n, ref in enumerate(sends)]

    @pl.when(c == 0)
    def _():
        sel = selector(ranks(groups(cols_ref[0:1, :], devices()[0] * SETS)))
        sel_ref[...] = sel
        ids_ref[...] = jnp.zeros((16, KG * B), BF16)
        ids_ref[:, :PAD] = sorted_order(sel).astype(BF16)
        begin(id_copies)

    sel = sel_ref[...]
    place = cols_ref[...] & 3
    weights = [
        [jnp.where(place[q:q + 1, :] == r, 1.0, 0.0).astype(BF16) for q in range(3)]
        for r in range(KG)
    ]
    for b in range(CHUNK):
        x = [p_ref[q, b] for q in range(3)]
        y = [x[0] * w[0] + x[1] * w[1] + x[2] * w[2] for w in weights]
        t = nt(sel, jnp.concatenate(y, axis=0))
        t0_ref[b * STRIDE:b * STRIDE + PAD, :] = t[:, :128]
        t1_ref[b * STRIDE:b * STRIDE + PAD, :] = t[:, 128:]
    for i in range(ROWS):
        pool_ref[i, quarter(c), :] = jnp.concatenate(
            [t[pl.ds(i, CHUNK, stride=STRIDE), :] for t in (t0_ref, t1_ref)], axis=1
        ).astype(BF16)
    begin(stores(c))

    @pl.when(c == QUARTERS - 1)
    def _():
        finished(id_copies)
        for done in range(QUARTERS):
            finished(stores(done))


def prolong(cols_t, p_t):
    def rows(n):
        return (QUARTERS * n + 1, CHUNK, KG * B), BF16

    return call(
        prolong_kernel, "prolong",
        [pl.BlockSpec((3, ROWS), lambda c: (0, 0)),
         pl.BlockSpec((3, CHUNK, B, ROWS), lambda c: (0, c, 0, 0))],
        [((ROWS, B, KG * B), BF16), rows(14), rows(14), rows(7), rows(21)],
        [
            pltpu.VMEM((PAD, ROWS), BF16),
            pltpu.VMEM((ROWS, B, KG * B), BF16),
            pltpu.VMEM((16, KG * B), BF16),
            pltpu.VMEM((CHUNK * STRIDE, 128), F32),
            pltpu.VMEM((CHUNK * STRIDE, 128), F32),
            pltpu.SemaphoreType.DMA((QUARTERS, 6)),
            pltpu.SemaphoreType.DMA((4,)),
        ],
        6_000_000_000, 8_000_000, 56, grid=(QUARTERS,),
    )(cols_t, p_t)


def set_name(slot):
    name = jnp.where(slot < 7, 0.0, 1.0)
    for start, value in ((14, 2.0), (28, 3.0), (42, 4.0), (56, 5.0), (70, 6.0), (84, 7.0),
                         (98, 8.0), (112, 0.0), (119, 1.0), (126, 9.0)):
        name = jnp.where(slot >= start, value, name)
    return name


def own_mask(src, key, sel):
    own = jnp.where(set_name(src) == key, 1.0, 0.0)
    by_row = nt(sel, own.astype(BF16)).astype(BF16)
    spread = jnp.where(iota((8, 8 * B), 1) >> 6 == iota((8, 8 * B), 0), 1.0, 0.0).astype(BF16)
    return jnp.dot(by_row, spread, preferred_element_type=F32)


def sorted_slots(src, sel):
    return nt(jnp.maximum(src, 0.0).astype(BF16), sel).astype(jnp.int32)


def merge_row(i, place, row, src_ref, mask_ref, a_ref, pool_ref, merged_ref):
    index = [src_ref[k, row] for k in range(7)]
    w = jnp.concatenate([pool_ref[j] for j in index] + [pool_ref[index[0]]], axis=0)
    a = a_ref[i]
    mask = jnp.broadcast_to(mask_ref[pl.ds(row, 1), :], a.shape).astype(BF16)
    a_own = a * mask
    both = jnp.concatenate([a_own, a - a_own], axis=0)
    merged = jnp.dot(both, w, preferred_element_type=F32).astype(BF16)
    merged_ref[place * B:place * B + B, :KG * B] = merged[:B]
    merged_ref[place * B:place * B + B, KG * B:] = merged[B:]


def order_slots(c_cols_ref, set_id, first_row, place_ref):
    for r in range(KG):
        for s in range(8):
            c = c_cols_ref[s, first_row + r]
            u = (c & 3) + jnp.where((c >> 2) == set_id, 0, 4)
            place_ref[r, u] = s


def store_blocks(total, first_row, place_ref, out_ref):
    total = total.astype(BF16)
    for r in range(KG):
        for u in range(8):
            out_ref[first_row + r, place_ref[r, u]] = total[r * B:(r + 1) * B, u * B:(u + 1) * B]


def one_set(s, set_base, src_ref, c_cols_ref, mask_ref, a_ref, pool_ref, merged_ref, place_ref,
            blocks_ref):
    first = s * FS
    order_slots(c_cols_ref, set_base + s, s * KG, place_ref)
    for i in range(FS):
        merge_row(first + i, i, first + i, src_ref, mask_ref, a_ref, pool_ref, merged_ref)
    own = pool_ref[pl.ds(first, FS)].reshape(FS * B, KG * B)
    store_blocks(tn(own, merged_ref[...]), s * KG, place_ref, blocks_ref)


def operator_kernel(c_cols_hbm, cols_hbm, a_cols_hbm, a_hbm, pool_hbm,
                    a_rows_hbm, a_next_hbm, out_hbm, local_hbm, flags_hbm, sel_hbm,
                    c_cols_ref, cols_ref, a_cols_ref, a_ref, rows_ref, pool_ref, blocks_ref, merged_ref,
                    mask_ref, local_ref, sel_ref, order_v, src_v, flag_v, order_ref, src_ref, flag_s,
                    place_ref, t0, t1, t2, t3, in_sems, sems, keep_sems, out_sems):
    def fetch(c):
        return pltpu.make_async_copy(a_hbm.at[:, quarter(c)], a_ref.at[:, quarter(c)], in_sems.at[c])

    small = load_all(((cols_hbm, cols_ref), (a_cols_hbm, a_cols_ref), (c_cols_hbm, c_cols_ref)), sems)
    begin(small)
    for c in range(QUARTERS):
        fetch(c).start()
    load = pltpu.make_async_copy(pool_hbm, pool_ref, sems.at[3])
    load.start()
    finished(small)

    device = devices()[0]
    set_base = device * SETS
    key = groups(cols_ref[0:1, :], set_base)
    rank = ranks(key)
    sel = selector(rank)
    sel_ref[...] = sel
    order_v[:, :PAD] = sorted_order(sel)[:8].astype(jnp.int32)
    order_v[:, PAD:] = jnp.zeros((8, 128 - PAD), jnp.int32)
    rank = to_column(rank) + 1.0
    row = iota((ROWS, ROWS), 0)
    sources = [
        jnp.sum(jnp.where(a_cols_ref[k:k + 1, :] - device * ROWS == row, rank, 0.0), axis=0,
                keepdims=True) - 1.0
        for k in range(7)
    ]
    src = jnp.concatenate(sources + [sources[0]], axis=0)
    keys = key.astype(F32)
    eight = iota((8, ROWS), 0)
    local_ref[...] = jnp.where(eight < 7, src, keys)
    away = jnp.max(jnp.where(src < 0.0, 1.0, 0.0), axis=0, keepdims=True)
    away = jnp.sum(jnp.where(eight.astype(F32) == keys, away, 0.0), axis=1, keepdims=True)
    name = jnp.where((src >= 0.0) & (keys == 1.0), set_name(src), 99.0)
    read = jnp.zeros((8, ROWS), F32)
    for k in range(7):
        read = read + jnp.where(name[k:k + 1, :] == eight.astype(F32), 1.0, 0.0)
    read = jnp.sum(read, axis=1, keepdims=True)
    flag_v[...] = jnp.where(iota((8, 128), 1) < 64, away, read).astype(jnp.int32)
    src_v[:, :PAD] = sorted_slots(src, sel)
    src_v[:, PAD:] = jnp.zeros((8, 128 - PAD), jnp.int32)
    mask_ref[...] = own_mask(src, keys, sel)
    to_smem = load_all(((order_v, order_ref), (src_v, src_ref), (flag_v, flag_s),
                        (local_ref, local_hbm), (flag_v, flags_hbm), (sel_ref, sel_hbm)),
                       sems.at[pl.ds(4, 6)])
    begin(to_smem)
    finished(to_smem)

    def keep(c, s):
        rows = pl.ds(s * FS, FS)
        return pltpu.make_async_copy(
            rows_ref.at[rows, quarter(c)], a_rows_hbm.at[rows, quarter(c)], keep_sems.at[c, s])

    def keep_next(c):
        return pltpu.make_async_copy(
            rows_ref.at[pl.ds(HALF, HALF), quarter(c)], a_next_hbm.at[:, quarter(c)],
            keep_sems.at[c, SETS])

    def later(s):
        return (flag_s[s + 1, 0] != 0) | (s == 0)

    t_refs = (t0, t1, t2, t3)

    def step(c, carry):
        fetch(c).wait()
        for a in range(CHUNK):
            zero = jnp.zeros((B, ROWS), BF16)
            x = [a_ref[k, c * CHUNK + a] for k in range(7)] + [zero]
            for h in range(4):
                pair = jnp.concatenate(x[2 * h:2 * h + 2], axis=0)
                t_refs[h][a * STRIDE:a * STRIDE + ROWS, :] = jnp.transpose(pair).astype(F32)
        for i in range(ROWS):
            rows_ref[i, quarter(c), :] = jnp.concatenate(
                [t[pl.ds(order_ref[0, i], CHUNK, stride=STRIDE), :] for t in t_refs], axis=1
            ).astype(BF16)

        def store(s, carry):
            @pl.when(later(s))
            def _():
                keep(c, s).start()
            return carry

        keep_next(c).start()
        return lax.fori_loop(0, SETS, store, carry)

    lax.fori_loop(0, QUARTERS, step, 0)
    load.wait()

    def store(s):
        rows = pl.ds(s * KG, KG)
        return pltpu.make_async_copy(blocks_ref.at[rows], out_hbm.at[rows], out_sems.at[s])

    def work(s, carry):
        @pl.when(flag_s[s + 1, 0] == 0)
        def _():
            one_set(s, set_base, src_ref, c_cols_ref, mask_ref, rows_ref, pool_ref, merged_ref,
                    place_ref, blocks_ref)
            store(s).start()
        return carry

    lax.fori_loop(1, SETS, work, 0)

    def end(s, carry):
        @pl.when(later(s))
        def _():
            finished([keep(c, s) for c in range(QUARTERS)])

        @pl.when(jnp.logical_not(later(s)))
        def _():
            store(s).wait()
        return carry

    lax.fori_loop(0, SETS, end, 0)
    finished([keep_next(c) for c in range(QUARTERS)])


def operator(c_cols_t, cols_t, a_cols_t, a_t, pool):
    return call(
        operator_kernel, "operator", [HBM] * 4 + [ANY],
        [((ROWS, B, 8 * B), BF16), ((HALF, B, 8 * B), BF16), ((SETS * KG, 8, B, B), BF16), ((8, ROWS), F32),
         ((8, 128), jnp.int32), ((PAD, ROWS), BF16)],
        [
            pltpu.SMEM((8, SETS * KG), jnp.int32),
            pltpu.VMEM((3, ROWS), jnp.int32),
            pltpu.VMEM((7, ROWS), jnp.int32),
            pltpu.VMEM((7, B, B, ROWS), BF16),
            pltpu.VMEM((ROWS, B, 8 * B), BF16),
            pltpu.VMEM((ROWS, B, KG * B), BF16),
            pltpu.VMEM((SETS * KG, 8, B, B), BF16),
            pltpu.VMEM((FS * B, 8 * B), BF16),
            pltpu.VMEM((PAD, 8 * B), F32),
            pltpu.VMEM((8, ROWS), F32),
            pltpu.VMEM((PAD, ROWS), BF16),
            pltpu.VMEM((8, 128), jnp.int32),
            pltpu.VMEM((8, 128), jnp.int32),
            pltpu.VMEM((8, 128), jnp.int32),
            pltpu.SMEM((8, 128), jnp.int32),
            pltpu.SMEM((8, 128), jnp.int32),
            pltpu.SMEM((8, 128), jnp.int32),
            pltpu.SMEM((KG, 8), jnp.int32),
        ] + [pltpu.VMEM((CHUNK * STRIDE, 128), F32)] * 4 + [
            pltpu.SemaphoreType.DMA((QUARTERS,)),
            pltpu.SemaphoreType.DMA((10,)),
            pltpu.SemaphoreType.DMA((QUARTERS, SETS + 1)),
            pltpu.SemaphoreType.DMA((SETS,)),
        ],
        4_000_000_000, 18_000_000, 53,
    )(c_cols_t, cols_t, a_cols_t, a_t, pool)


def pool_copies(parts, pool_ref, sems):
    copies = []
    start = ROWS
    for n, part in enumerate(parts):
        rows = (part.shape[0] - 1) // QUARTERS
        for c in range(QUARTERS):
            copies.append(pltpu.make_async_copy(
                part.at[pl.ds(c * rows, rows)],
                pool_ref.at[pl.ds(start, rows), pl.ds(c * CHUNK, CHUNK)],
                sems.at[n, c],
            ))
        start += rows
    return copies


def straddle_kernel(a_cols_hbm, local_hbm, flags_hbm, sel_hbm, a_next_hbm, pool_hbm, *refs):
    parts = refs[:4]
    (out_hbm, src_hbm, mask_hbm, a_cols_ref, local_ref, flag_ref, sel_ref, pool_ref, rows_ref,
     names_ref, merged_ref, partial_ref, mask_ref, src_v, src_ref, sems, pool_sems, small_sems) = refs[4:]
    small = load_all(
        [(flags_hbm, flag_ref), (a_cols_hbm, a_cols_ref), (local_hbm, local_ref), (sel_hbm, sel_ref)]
        + [(part.at[part.shape[0] - 1], names_ref.at[n]) for n, part in enumerate(parts)], small_sems)
    begin(small)
    loads = pool_copies(parts, pool_ref, sems)
    loads.append(pltpu.make_async_copy(a_next_hbm, rows_ref, small_sems.at[8]))
    begin(loads)
    finished(small)
    ids = devices()

    def unit(u):
        first, rows = (0, 7) if u == 0 else (7, 7) if u == 1 else ((u - 1) * FS, FS)
        return pltpu.make_async_copy(
            pool_hbm.at[pl.ds(first, rows)], pool_ref.at[pl.ds(first, rows)], pool_sems.at[u])

    def read(u):
        return (flag_ref[u, 64] != 0) | (u == 1)

    for u in range(7):
        @pl.when(read(u))
        def _(u=u):
            unit(u).start()

    shifts = (((70, 84, 84 - 70),), ((56, 70, 98 - 56),), ((7, 14, 112 - 7),),
              ((0, 7, 119), (14, 28, 126 - 14)))
    near = ((64, 88), (56, 72), (0, 16), (0, 32))
    found = [jnp.zeros((1, ROWS), F32)] * 7
    for n in range(4):
        low, high = near[n]
        column = jnp.transpose(names_ref[n][:, :128].astype(F32))[low:high, 0:1].astype(jnp.int32)
        row = iota((high - low, 1), 0) + low
        slot = jnp.zeros((high - low, 1), jnp.int32)
        for first, last, shift in shifts[n]:
            slot = jnp.where((row >= first) & (row < last), row + shift + 1, slot)
        column = jnp.where(slot > 0, column + ids[n + 1] * ROWS, -1)
        slot = slot.astype(F32)
        for k in range(7):
            found[k] = found[k] + jnp.sum(
                jnp.where(a_cols_ref[k:k + 1, :] == column, slot, 0.0), axis=0, keepdims=True)
    local = local_ref[...]
    away = jnp.concatenate(found + [found[0]], axis=0) - 1.0
    src = jnp.where(local >= 0.0, local, away)
    src = jnp.where(iota((8, ROWS), 0) < 7, src, jnp.broadcast_to(src[0:1, :], (8, ROWS)))
    sel = sel_ref[...]
    src_v[:, :PAD] = sorted_slots(src, sel)
    src_v[:, PAD:] = jnp.zeros((8, 128 - PAD), jnp.int32)
    out = load_all(((src_v, src_ref), (src_v, src_hbm), (mask_ref, mask_hbm)),
                   small_sems.at[pl.ds(9, 3)])
    begin(out[:2])
    mask_ref[...] = own_mask(src, local[7:8, :], sel)
    out[2].start()
    finished(out[:1] + loads)
    for u in range(7):
        @pl.when(read(u))
        def _(u=u):
            unit(u).wait()
    for i in range(HALF):
        merge_row(i, i, HALF + i, src_ref, mask_ref, rows_ref, pool_ref, merged_ref)
    own = pool_ref[HALF:FS].reshape(HALF * B, KG * B)
    partial_ref[...] = tn(own, merged_ref[...]).astype(BF16)
    last = pltpu.make_async_copy(partial_ref, out_hbm, small_sems.at[12])
    last.start()
    finished(out[1:] + [last])


def straddle(a_cols_t, local, flags, sel, a_next, pool, parts):
    return call(
        straddle_kernel, "straddle", [HBM] + [ANY] * 9,
        [((KG * B, 8 * B), BF16), ((8, 128), jnp.int32), ((PAD, 8 * B), F32)],
        [
            pltpu.VMEM((7, ROWS), jnp.int32),
            pltpu.VMEM((8, ROWS), F32),
            pltpu.SMEM((8, 128), jnp.int32),
            pltpu.VMEM((PAD, ROWS), BF16),
            pltpu.VMEM((POOL, B, KG * B), BF16),
            pltpu.VMEM((HALF, B, 8 * B), BF16),
            pltpu.VMEM((4, 16, KG * B), BF16),
            pltpu.VMEM((HALF * B, 8 * B), BF16),
            pltpu.VMEM((KG * B, 8 * B), BF16),
            pltpu.VMEM((PAD, 8 * B), F32),
            pltpu.VMEM((8, 128), jnp.int32),
            pltpu.SMEM((8, 128), jnp.int32),
            pltpu.SemaphoreType.DMA((4, QUARTERS)),
            pltpu.SemaphoreType.DMA((7,)),
            pltpu.SemaphoreType.DMA((13,)),
        ],
        300_000_000, 6_000_000, 14,
    )(a_cols_t, local, flags, sel, a_next, pool, *parts)


def sets_kernel(src_hbm, flags_hbm, c_cols_hbm, mask_hbm, a_rows_hbm, pool_hbm, *refs):
    parts = refs[:4]
    (_, out_hbm, first_hbm, src_ref, flag_ref, c_cols_ref, mask_ref, first_ref, pool_ref, rows_ref,
     blocks_ref, merged_ref, place_ref, small_sems, sems, row_sems, out_sems) = refs[4:]
    small = load_all(((flags_hbm, flag_ref), (src_hbm, src_ref), (c_cols_hbm, c_cols_ref),
                      (mask_hbm, mask_ref)), small_sems)
    begin(small)
    loads = pool_copies(parts, pool_ref, sems) + [
        pltpu.make_async_copy(pool_hbm, pool_ref.at[pl.ds(0, ROWS)], small_sems.at[4])]
    set_base = devices()[0] * SETS

    def fetch(s):
        rows = pl.ds(s * FS, FS)
        return pltpu.make_async_copy(a_rows_hbm.at[rows], rows_ref.at[rows], row_sems.at[s])

    def store(s):
        rows = pl.ds(s * KG, KG)
        return pltpu.make_async_copy(blocks_ref.at[rows], out_hbm.at[rows], out_sems.at[s])

    def here(s):
        return flag_ref[s + 1, 0] != 0

    fetch(0).start()
    begin(loads)
    finished(small)
    for s in range(1, SETS):
        @pl.when(here(s))
        def _(s=s):
            fetch(s).start()
    fetch(0).wait()
    finished(loads)
    for i in range(HALF):
        merge_row(i, i, i, src_ref, mask_ref, rows_ref, pool_ref, merged_ref)
    own = pool_ref[:HALF].reshape(HALF * B, KG * B)
    first_ref[...] = tn(own, merged_ref[:HALF * B, :])
    first = pltpu.make_async_copy(first_ref, first_hbm, small_sems.at[5])
    first.start()

    def work(s, carry):
        @pl.when(here(s))
        def _():
            fetch(s).wait()
            one_set(s, set_base, src_ref, c_cols_ref, mask_ref, rows_ref, pool_ref, merged_ref,
                    place_ref, blocks_ref)
            store(s).start()
        return carry

    lax.fori_loop(1, SETS, work, 0)

    def end(s, carry):
        @pl.when(here(s))
        def _():
            store(s).wait()
        return carry

    lax.fori_loop(1, SETS, end, 0)
    first.wait()


def sets(src, flags, c_cols_t, mask, a_rows, pool, parts, whole):
    return call(
        sets_kernel, "sets", [ANY] * 2 + [HBM] + [ANY] * 8,
        [((SETS * KG, 8, B, B), BF16), ((KG * B, 8 * B), F32)],
        [
            pltpu.SMEM((8, 128), jnp.int32),
            pltpu.SMEM((8, 128), jnp.int32),
            pltpu.SMEM((8, SETS * KG), jnp.int32),
            pltpu.VMEM((PAD, 8 * B), F32),
            pltpu.VMEM((KG * B, 8 * B), F32),
            pltpu.VMEM((POOL, B, KG * B), BF16),
            pltpu.VMEM((ROWS, B, 8 * B), BF16),
            pltpu.VMEM((SETS * KG, 8, B, B), BF16),
            pltpu.VMEM((FS * B, 8 * B), BF16),
            pltpu.SMEM((KG, 8), jnp.int32),
            pltpu.SemaphoreType.DMA((6,)),
            pltpu.SemaphoreType.DMA((4, QUARTERS)),
            pltpu.SemaphoreType.DMA((SETS,)),
            pltpu.SemaphoreType.DMA((SETS,)),
        ],
        2_500_000_000, 12_000_000, 48, aliases={10: 0},
    )(src, flags, c_cols_t, mask, a_rows, pool, *parts, whole)


def finish_kernel(c_cols_hbm, first_hbm, incoming_hbm, _, out_hbm, c_cols_ref, first_ref, incoming_ref,
                  blocks_ref, place_ref, sems):
    loads = load_all(((c_cols_hbm, c_cols_ref), (first_hbm, first_ref), (incoming_hbm, incoming_ref)),
                     sems)
    begin(loads)
    finished(loads[:1])
    order_slots(c_cols_ref, devices()[0] * SETS, 0, place_ref)
    finished(loads[1:])
    store_blocks(first_ref[...] + incoming_ref[...].astype(F32), 0, place_ref, blocks_ref)
    copy = pltpu.make_async_copy(blocks_ref, out_hbm.at[pl.ds(0, KG)], sems.at[3])
    copy.start()
    copy.wait()


def finish(c_cols_t, first, incoming, whole):
    return call(
        finish_kernel, "finish", [HBM] + [ANY] * 3, [((SETS * KG, 8, B, B), BF16)],
        [
            pltpu.SMEM((8, SETS * KG), jnp.int32),
            pltpu.VMEM((KG * B, 8 * B), F32),
            pltpu.VMEM((KG * B, 8 * B), BF16),
            pltpu.VMEM((KG, 8, B, B), BF16),
            pltpu.SMEM((KG, 8), jnp.int32),
            pltpu.SemaphoreType.DMA((4,)),
        ],
        1_000_000, 1_500_000, 6, aliases={3: 0},
    )(c_cols_t, first, incoming, whole)[0]


def shards(a_blocks, a_cols, p_blocks, p_cols, c_cols):
    cols_t, a_cols_t, c_cols_t = p_cols.T, a_cols.T, c_cols.T
    moves = (("dom", 1), ("dom", -1), ("sub", 1), ("sub", -1))
    pool, *sends = prolong(cols_t, p_blocks.transpose(1, 2, 3, 0))
    parts = [passed_along(rows, axis, step) for rows, (axis, step) in zip(sends, moves)]
    a_rows, a_next, whole, local, flags, sel = operator(
        c_cols_t, cols_t, a_cols_t, a_blocks.transpose(1, 2, 3, 0), pool)
    partial, src, mask = straddle(a_cols_t, local, flags, sel, a_next, pool, parts)
    incoming = passed_along(partial, "sub", 1)
    whole, first = sets(src, flags, c_cols_t, mask, a_rows, pool, parts, whole)
    return finish(c_cols_t, first, incoming, whole)


def solution(mesh):
    spec4 = P(("dom", "sub"), None, None, None)
    spec2 = P(("dom", "sub"), None)
    return jax.shard_map(
        shards, mesh=mesh, in_specs=(spec4, spec2, spec4, spec2, spec2), out_specs=spec4,
        check_vma=False,
    )
```

```python
import jax
import jax.numpy as jnp
from jax import lax
from jax.experimental import pallas as pl
from jax.experimental.pallas import tpu as pltpu
from jax.sharding import PartitionSpec as P

KG = 4
FS = 14
HALF = FS // 2
ROWS = 84
PAD = 88
SETS = 6
B = 64
POOL = ROWS + FS + FS + HALF + HALF + FS
F32 = jnp.float32
BF16 = jnp.bfloat16


def passed_along(block, axis, distance):
    n = lax.axis_size(axis)
    return lax.ppermute(block, axis, [((i - distance) % n, i) for i in range(n)])


def iota(shape, dim):
    return lax.broadcasted_iota(jnp.int32, shape, dim)


QUARTERS = 4
CHUNK = B // QUARTERS
STRIDE = 89
SENDS = (((70, 14),), ((56, 14),), ((7, 7),))
BACK = HALF + FS
NARROW = BACK + (BACK + 1) // 2
AFTER = POOL - BACK
ANY = pl.BlockSpec(memory_space=pl.ANY)
HBM = pl.BlockSpec(memory_space=pltpu.HBM)


def call(kernel, name, ins, outs, scratch, flops, nbytes, vmem, aliases=None, grid=()):
    return pl.pallas_call(
        kernel,
        grid=grid,
        in_specs=ins,
        out_specs=[ANY] * len(outs),
        out_shape=[jax.ShapeDtypeStruct(*shape) for shape in outs],
        scratch_shapes=scratch,
        input_output_aliases=aliases or {},
        compiler_params=pltpu.CompilerParams(vmem_limit_bytes=vmem * 1024 * 1024),
        cost_estimate=pl.CostEstimate(flops=flops, bytes_accessed=nbytes, transcendentals=0),
        name=name,
    )


def devices():
    dom_count, sub_count = lax.axis_size("dom"), lax.axis_size("sub")
    dom, sub = lax.axis_index("dom"), lax.axis_index("sub")

    def number(d, s):
        return lax.rem(d, dom_count) * sub_count + lax.rem(s, sub_count)

    return [number(dom, sub), number(dom + dom_count - 1, sub), number(dom + 1, sub),
            number(dom, sub + sub_count - 1), number(dom, sub + 1)]


def begin(copies):
    for copy in copies:
        copy.start()


def finished(copies):
    for copy in copies:
        copy.wait()


def load_all(pairs, sems):
    return [pltpu.make_async_copy(src, dst, sems.at[n]) for n, (src, dst) in enumerate(pairs)]


def groups(lead, set_base):
    group = (lead >> 2) - set_base
    own = (group >= 0) & (group < SETS)
    return jnp.where(own, jnp.where(group > 0, group + 1, 0), 1)


def to_column(row):
    wide = jnp.broadcast_to(row, (ROWS, ROWS))
    diagonal = iota((ROWS, ROWS), 0) == iota((ROWS, ROWS), 1)
    return jnp.sum(jnp.where(diagonal, wide, 0.0), axis=1, keepdims=True)


def ranks(key):
    order = (key * 128 + iota((1, ROWS), 1)).astype(F32)
    return jnp.sum(jnp.where(to_column(order) < order, 1.0, 0.0), axis=0, keepdims=True)


def selector(rank):
    return jnp.where(rank.astype(jnp.int32) == iota((PAD, ROWS), 0), 1.0, 0.0).astype(BF16)


def sorted_order(sel):
    return nt(iota((16, ROWS), 1).astype(F32).astype(BF16), sel)


def nt(x, y):
    return lax.dot_general(x, y, (((1,), (1,)), ((), ())), preferred_element_type=F32)


def tn(x, y):
    return lax.dot_general(x, y, (((0,), (0,)), ((), ())), preferred_element_type=F32)


def quarter(c):
    return pl.ds(pl.multiple_of(c * CHUNK, CHUNK), CHUNK)


def send_copies(c, pool_ref, send_refs, sems):
    copies = []
    for ref, runs in zip(send_refs, SENDS):
        total = sum(n for _, n in runs)
        done = 0
        for first, n in runs:
            copies.append(pltpu.make_async_copy(
                pool_ref.at[pl.ds(first, n), quarter(c)],
                ref.at[pl.ds(c * total + done, n)],
                sems.at[c, len(copies)],
            ))
            done += n
    return copies


def prolong_kernel(cols_ref, p_ref, pool_hbm, up_hbm, down_hbm, fore_hbm, back_hbm,
                   sel_ref, back_sel_ref, pool_ref, back_ref, ids_ref, back_ids_ref,
                   t0_ref, t1_ref, t2_ref, t3_ref, out_sems, id_sems):
    c = pl.program_id(0)
    sends = (up_hbm, down_hbm, fore_hbm)

    def stores(c):
        whole = pltpu.make_async_copy(
            pool_ref.at[:, quarter(c)], pool_hbm.at[:, quarter(c)], out_sems.at[c, 5])
        rows = pl.ds(c * NARROW, NARROW)
        back = pltpu.make_async_copy(back_ref.at[rows], back_hbm.at[rows], out_sems.at[c, 4])
        return [back] + send_copies(c, pool_ref, sends, out_sems) + [whole]

    id_copies = [pltpu.make_async_copy(ids_ref, ref.at[ref.shape[0] - 1], id_sems.at[n])
                 for n, ref in enumerate(sends)]
    id_copies.append(pltpu.make_async_copy(
        back_ids_ref, back_hbm.at[back_hbm.shape[0] - 1], id_sems.at[3]))

    @pl.when(c == 0)
    def _():
        rank = ranks(groups(cols_ref[0:1, :], devices()[0] * SETS))
        sel = selector(rank)
        sel_ref[...] = sel
        back_rank = jnp.where(rank < 7.0, rank, jnp.where((rank >= 14.0) & (rank < 28.0), rank - 7.0, 99.0))
        back_sel_ref[...] = jnp.where(
            back_rank.astype(jnp.int32) == iota((32, ROWS), 0), 1.0, 0.0).astype(BF16)
        notes = iota((16, ROWS), 1)
        for q in range(3):
            notes = jnp.where(iota((16, ROWS), 0) == q + 1, cols_ref[q:q + 1, :] & 3, notes)
        notes = nt(notes.astype(F32).astype(BF16), sel).astype(BF16)
        ids_ref[...] = jnp.zeros((16, KG * B), BF16)
        ids_ref[:, :PAD] = notes
        back_ids_ref[...] = jnp.zeros((16, 128), BF16)
        back_ids_ref[:, :PAD] = notes
        begin(id_copies)

    sel = sel_ref[...]
    back_sel = back_sel_ref[...]
    place = cols_ref[...] & 3
    weights = [
        [jnp.where(place[q:q + 1, :] == r, 1.0, 0.0).astype(BF16) for q in range(3)]
        for r in range(KG)
    ]
    for b in range(CHUNK):
        x = [p_ref[q, b] for q in range(3)]
        y = [x[0] * w[0] + x[1] * w[1] + x[2] * w[2] for w in weights]
        t = nt(sel, jnp.concatenate(y, axis=0))
        t0_ref[b * STRIDE:b * STRIDE + PAD, :] = t[:, :128]
        t1_ref[b * STRIDE:b * STRIDE + PAD, :] = t[:, 128:]
        t = nt(back_sel, jnp.concatenate(x + [x[2]], axis=0))
        t2_ref[b * 33:b * 33 + 32, :] = t[:, :128]
        t3_ref[b * 33:b * 33 + 32, :] = t[:, 128:]
    left = iota((CHUNK, 128), 1) < B
    for m in range(BACK):
        back_ref[c * NARROW + m] = t2_ref[pl.ds(m, CHUNK, stride=33), :].astype(BF16)
    for m in range(0, BACK, 2):
        back_ref[c * NARROW + BACK + m // 2] = jnp.where(
            left, t3_ref[pl.ds(m, CHUNK, stride=33), :], t3_ref[pl.ds(m + 1, CHUNK, stride=33), :]
        ).astype(BF16)
    for i in range(ROWS):
        pool_ref[i, quarter(c), :] = jnp.concatenate(
            [t[pl.ds(i, CHUNK, stride=STRIDE), :] for t in (t0_ref, t1_ref)], axis=1
        ).astype(BF16)
    begin(stores(c))

    @pl.when(c == QUARTERS - 1)
    def _():
        finished(id_copies)
        for done in range(QUARTERS):
            finished(stores(done))


def prolong(cols_t, p_t):
    def rows(n):
        return (QUARTERS * n + 1, CHUNK, KG * B), BF16

    return call(
        prolong_kernel, "prolong",
        [pl.BlockSpec((3, ROWS), lambda c: (0, 0)),
         pl.BlockSpec((3, CHUNK, B, ROWS), lambda c: (0, c, 0, 0))],
        [((ROWS, B, KG * B), BF16), rows(14), rows(14), rows(7),
         ((QUARTERS * NARROW + 1, CHUNK, 128), BF16)],
        [
            pltpu.VMEM((PAD, ROWS), BF16),
            pltpu.VMEM((32, ROWS), BF16),
            pltpu.VMEM((ROWS, B, KG * B), BF16),
            pltpu.VMEM((QUARTERS * NARROW, CHUNK, 128), BF16),
            pltpu.VMEM((16, KG * B), BF16),
            pltpu.VMEM((16, 128), BF16),
            pltpu.VMEM((CHUNK * STRIDE, 128), F32),
            pltpu.VMEM((CHUNK * STRIDE, 128), F32),
            pltpu.VMEM((CHUNK * 33, 128), F32),
            pltpu.VMEM((CHUNK * 33, 128), F32),
            pltpu.SemaphoreType.DMA((QUARTERS, 6)),
            pltpu.SemaphoreType.DMA((4,)),
        ],
        6_000_000_000, 8_000_000, 56, grid=(QUARTERS,),
    )(cols_t, p_t)


def set_name(slot):
    name = jnp.where(slot < 7, 0.0, 1.0)
    for start, value in ((14, 2.0), (28, 3.0), (42, 4.0), (56, 5.0), (70, 6.0), (84, 7.0),
                         (98, 8.0), (112, 0.0), (119, 1.0), (126, 9.0)):
        name = jnp.where(slot >= start, value, name)
    return name


def own_mask(src, key, sel):
    own = jnp.where(set_name(src) == key, 1.0, 0.0)
    by_row = nt(sel, own.astype(BF16)).astype(BF16)
    spread = jnp.where(iota((8, 8 * B), 1) >> 6 == iota((8, 8 * B), 0), 1.0, 0.0).astype(BF16)
    return jnp.dot(by_row, spread, preferred_element_type=F32)


def sorted_slots(src, sel):
    return nt(jnp.maximum(src, 0.0).astype(BF16), sel).astype(jnp.int32)


def merge_row(i, place, row, src_ref, mask_ref, a_ref, pool_ref, merged_ref):
    index = [src_ref[k, row] for k in range(7)]
    w = jnp.concatenate([pool_ref[j] for j in index] + [pool_ref[index[0]]], axis=0)
    a = a_ref[i]
    mask = jnp.broadcast_to(mask_ref[pl.ds(row, 1), :], a.shape).astype(BF16)
    a_own = a * mask
    both = jnp.concatenate([a_own, a - a_own], axis=0)
    merged = jnp.dot(both, w, preferred_element_type=F32).astype(BF16)
    merged_ref[place * B:place * B + B, :KG * B] = merged[:B]
    merged_ref[place * B:place * B + B, KG * B:] = merged[B:]


def slot_places(c_cols, set_base):
    row = iota(c_cols.shape, 1)
    u = (c_cols & 3) + jnp.where((c_cols >> 2) == set_base + (row >> 2), 0, 4)
    place = jnp.zeros(c_cols.shape, jnp.int32)
    for slot in range(8):
        place = place + jnp.where(u[slot:slot + 1, :] == iota(c_cols.shape, 0), slot, 0)
    return place


def store_blocks(total, first_row, place_ref, out_ref):
    total = total.astype(BF16)
    for r in range(KG):
        for u in range(8):
            out_ref[first_row + r, place_ref[u, first_row + r]] = total[r * B:(r + 1) * B, u * B:(u + 1) * B]


def one_set(s, src_ref, mask_ref, a_ref, pool_ref, merged_ref, place_ref, blocks_ref):
    first = s * FS
    for i in range(FS):
        merge_row(first + i, i, first + i, src_ref, mask_ref, a_ref, pool_ref, merged_ref)
    own = pool_ref[pl.ds(first, FS)].reshape(FS * B, KG * B)
    store_blocks(tn(own, merged_ref[...]), s * KG, place_ref, blocks_ref)


def operator_kernel(c_cols_hbm, cols_hbm, a_cols_hbm, a_hbm, pool_hbm,
                    a_rows_hbm, a_next_hbm, out_hbm, local_hbm, flags_hbm, sel_hbm, places_hbm,
                    c_cols_ref, cols_ref, a_cols_ref, a_ref, rows_ref, pool_ref, blocks_ref, merged_ref,
                    mask_ref, local_ref, sel_ref, order_v, src_v, flag_v, place_v, order_ref, src_ref, flag_s,
                    place_ref, t0, t1, t2, t3, in_sems, sems, keep_sems, out_sems):
    def fetch(c):
        return pltpu.make_async_copy(a_hbm.at[:, quarter(c)], a_ref.at[:, quarter(c)], in_sems.at[c])

    small = load_all(((cols_hbm, cols_ref), (a_cols_hbm, a_cols_ref), (c_cols_hbm, c_cols_ref)), sems)
    begin(small)
    for c in range(QUARTERS):
        fetch(c).start()
    load = pltpu.make_async_copy(pool_hbm, pool_ref, sems.at[3])
    load.start()
    finished(small)

    device = devices()[0]
    set_base = device * SETS
    key = groups(cols_ref[0:1, :], set_base)
    rank = ranks(key)
    sel = selector(rank)
    sel_ref[...] = sel
    order_v[:, :PAD] = sorted_order(sel)[:8].astype(jnp.int32)
    order_v[:, PAD:] = jnp.zeros((8, 128 - PAD), jnp.int32)
    rank = to_column(rank) + 1.0
    row = iota((ROWS, ROWS), 0)
    sources = [
        jnp.sum(jnp.where(a_cols_ref[k:k + 1, :] - device * ROWS == row, rank, 0.0), axis=0,
                keepdims=True) - 1.0
        for k in range(7)
    ]
    src = jnp.concatenate(sources + [sources[0]], axis=0)
    keys = key.astype(F32)
    eight = iota((8, ROWS), 0)
    local_ref[...] = jnp.where(eight < 7, src, keys)
    away = jnp.max(jnp.where(src < 0.0, 1.0, 0.0), axis=0, keepdims=True)
    away = jnp.sum(jnp.where(eight.astype(F32) == keys, away, 0.0), axis=1, keepdims=True)
    name = jnp.where((src >= 0.0) & (keys == 1.0), set_name(src), 99.0)
    read = jnp.zeros((8, ROWS), F32)
    for k in range(7):
        read = read + jnp.where(name[k:k + 1, :] == eight.astype(F32), 1.0, 0.0)
    read = jnp.sum(read, axis=1, keepdims=True)
    flag_v[...] = jnp.where(iota((8, 128), 1) < 64, away, read).astype(jnp.int32)
    src_v[:, :PAD] = sorted_slots(src, sel)
    src_v[:, PAD:] = jnp.zeros((8, 128 - PAD), jnp.int32)
    place_v[:, :SETS * KG] = slot_places(c_cols_ref[...], set_base)
    place_v[:, SETS * KG:] = jnp.zeros((8, 128 - SETS * KG), jnp.int32)
    mask_ref[...] = own_mask(src, keys, sel)
    to_smem = load_all(((order_v, order_ref), (src_v, src_ref), (flag_v, flag_s),
                        (place_v, place_ref), (local_ref, local_hbm), (flag_v, flags_hbm),
                        (sel_ref, sel_hbm), (place_v, places_hbm)),
                       sems.at[pl.ds(4, 8)])
    begin(to_smem)

    def keep(c, s):
        rows = pl.ds(s * FS, FS)
        return pltpu.make_async_copy(
            rows_ref.at[rows, quarter(c)], a_rows_hbm.at[rows, quarter(c)], keep_sems.at[c, s])

    def keep_next(c):
        return pltpu.make_async_copy(
            rows_ref.at[pl.ds(HALF, HALF), quarter(c)], a_next_hbm.at[:, quarter(c)],
            keep_sems.at[c, SETS])

    def later(s):
        return (flag_s[s + 1, 0] != 0) | (s == 0)

    t_refs = (t0, t1, t2, t3)

    def step(c, carry):
        fetch(c).wait()
        for a in range(CHUNK):
            zero = jnp.zeros((B, ROWS), BF16)
            x = [a_ref[k, c * CHUNK + a] for k in range(7)] + [zero]
            for h in range(4):
                pair = jnp.concatenate(x[2 * h:2 * h + 2], axis=0)
                t_refs[h][a * STRIDE:a * STRIDE + ROWS, :] = jnp.transpose(pair).astype(F32)

        @pl.when(c == 0)
        def _():
            finished(to_smem)

        for i in range(ROWS):
            rows_ref[i, quarter(c), :] = jnp.concatenate(
                [t[pl.ds(order_ref[0, i], CHUNK, stride=STRIDE), :] for t in t_refs], axis=1
            ).astype(BF16)

        def store(s, carry):
            @pl.when(later(s))
            def _():
                keep(c, s).start()
            return carry

        keep_next(c).start()
        return lax.fori_loop(0, SETS, store, carry)

    lax.fori_loop(0, QUARTERS, step, 0)
    load.wait()

    def store(s):
        rows = pl.ds(s * KG, KG)
        return pltpu.make_async_copy(blocks_ref.at[rows], out_hbm.at[rows], out_sems.at[s])

    def work(s, carry):
        @pl.when(flag_s[s + 1, 0] == 0)
        def _():
            one_set(s, src_ref, mask_ref, rows_ref, pool_ref, merged_ref, place_ref, blocks_ref)
            store(s).start()
        return carry

    lax.fori_loop(1, SETS, work, 0)

    def end(s, carry):
        @pl.when(later(s))
        def _():
            finished([keep(c, s) for c in range(QUARTERS)])

        @pl.when(jnp.logical_not(later(s)))
        def _():
            store(s).wait()
        return carry

    lax.fori_loop(0, SETS, end, 0)
    finished([keep_next(c) for c in range(QUARTERS)])


def operator(c_cols_t, cols_t, a_cols_t, a_t, pool):
    return call(
        operator_kernel, "operator", [HBM] * 4 + [ANY],
        [((ROWS, B, 8 * B), BF16), ((HALF, B, 8 * B), BF16), ((SETS * KG, 8, B, B), BF16), ((8, ROWS), F32),
         ((8, 128), jnp.int32), ((PAD, ROWS), BF16), ((8, 128), jnp.int32)],
        [
            pltpu.VMEM((8, SETS * KG), jnp.int32),
            pltpu.VMEM((3, ROWS), jnp.int32),
            pltpu.VMEM((7, ROWS), jnp.int32),
            pltpu.VMEM((7, B, B, ROWS), BF16),
            pltpu.VMEM((ROWS, B, 8 * B), BF16),
            pltpu.VMEM((ROWS, B, KG * B), BF16),
            pltpu.VMEM((SETS * KG, 8, B, B), BF16),
            pltpu.VMEM((FS * B, 8 * B), BF16),
            pltpu.VMEM((PAD, 8 * B), F32),
            pltpu.VMEM((8, ROWS), F32),
            pltpu.VMEM((PAD, ROWS), BF16),
            pltpu.VMEM((8, 128), jnp.int32),
            pltpu.VMEM((8, 128), jnp.int32),
            pltpu.VMEM((8, 128), jnp.int32),
            pltpu.VMEM((8, 128), jnp.int32),
            pltpu.SMEM((8, 128), jnp.int32),
            pltpu.SMEM((8, 128), jnp.int32),
            pltpu.SMEM((8, 128), jnp.int32),
            pltpu.SMEM((8, 128), jnp.int32),
        ] + [pltpu.VMEM((CHUNK * STRIDE, 128), F32)] * 4 + [
            pltpu.SemaphoreType.DMA((QUARTERS,)),
            pltpu.SemaphoreType.DMA((12,)),
            pltpu.SemaphoreType.DMA((QUARTERS, SETS + 1)),
            pltpu.SemaphoreType.DMA((SETS,)),
        ],
        4_000_000_000, 18_000_000, 53,
    )(c_cols_t, cols_t, a_cols_t, a_t, pool)


def pool_copies(parts, pool_ref, sems):
    copies = []
    start = ROWS
    for n, part in enumerate(parts):
        rows = (part.shape[0] - 1) // QUARTERS
        for c in range(QUARTERS):
            copies.append(pltpu.make_async_copy(
                part.at[pl.ds(c * rows, rows)],
                pool_ref.at[pl.ds(start, rows), pl.ds(c * CHUNK, CHUNK)],
                sems.at[n, c],
            ))
        start += rows
    return copies


def straddle_kernel(a_cols_hbm, local_hbm, flags_hbm, sel_hbm, a_next_hbm, pool_hbm, *refs):
    *parts, back_hbm = refs[:4]
    (out_hbm, src_hbm, mask_hbm, after_hbm, a_cols_ref, local_ref, flag_ref, sel_ref, pool_ref, rows_ref,
     names_ref, back_names_ref, narrow_ref, merged_ref, partial_ref, mask_ref, src_v, src_ref, places_v,
     places_ref, sems, pool_sems, small_sems) = refs[4:]
    small = load_all(
        [(flags_hbm, flag_ref), (a_cols_hbm, a_cols_ref), (local_hbm, local_ref), (sel_hbm, sel_ref)]
        + [(part.at[part.shape[0] - 1], names_ref.at[n]) for n, part in enumerate(parts)]
        + [(back_hbm.at[back_hbm.shape[0] - 1], back_names_ref)], small_sems)
    begin(small)
    loads = pool_copies(parts, pool_ref, sems)
    loads.append(pltpu.make_async_copy(a_next_hbm, rows_ref, small_sems.at[8]))
    narrow = [
        pltpu.make_async_copy(back_hbm.at[pl.ds(c * NARROW, NARROW)],
                              narrow_ref.at[:, pl.ds(c * CHUNK, CHUNK)], sems.at[3, c])
        for c in range(QUARTERS)
    ]
    begin(narrow + loads)
    finished(small)
    places_v[...] = back_names_ref[...].astype(F32).astype(jnp.int32)
    places = pltpu.make_async_copy(places_v, places_ref, small_sems.at[13])
    places.start()
    ids = devices()

    def unit(u):
        first, rows = (0, 7) if u == 0 else (7, 7) if u == 1 else ((u - 1) * FS, FS)
        return pltpu.make_async_copy(
            pool_hbm.at[pl.ds(first, rows)], pool_ref.at[pl.ds(first, rows)], pool_sems.at[u])

    def read(u):
        return (flag_ref[u, 64] != 0) | (u == 1)

    for u in range(7):
        @pl.when(read(u))
        def _(u=u):
            unit(u).start()

    shifts = (((70, 84, 84 - 70),), ((56, 70, 98 - 56),), ((7, 14, 112 - 7),),
              ((0, 7, 119), (14, 28, 126 - 14)))
    near = ((64, 88), (56, 72), (0, 16), (0, 32))
    found = [jnp.zeros((1, ROWS), F32)] * 7
    for n in range(4):
        low, high = near[n]
        name = names_ref[n][:, :128] if n < 3 else back_names_ref[...]
        column = jnp.transpose(name.astype(F32))[low:high, 0:1].astype(jnp.int32)
        row = iota((high - low, 1), 0) + low
        slot = jnp.zeros((high - low, 1), jnp.int32)
        for first, last, shift in shifts[n]:
            slot = jnp.where((row >= first) & (row < last), row + shift + 1, slot)
        column = jnp.where(slot > 0, column + ids[n + 1] * ROWS, -1)
        slot = slot.astype(F32)
        for k in range(7):
            found[k] = found[k] + jnp.sum(
                jnp.where(a_cols_ref[k:k + 1, :] == column, slot, 0.0), axis=0, keepdims=True)
    local = local_ref[...]
    away = jnp.concatenate(found + [found[0]], axis=0) - 1.0
    src = jnp.where(local >= 0.0, local, away)
    src = jnp.where(iota((8, ROWS), 0) < 7, src, jnp.broadcast_to(src[0:1, :], (8, ROWS)))
    sel = sel_ref[...]
    src_v[:, :PAD] = sorted_slots(src, sel)
    src_v[:, PAD:] = jnp.zeros((8, 128 - PAD), jnp.int32)
    out = load_all(((src_v, src_ref), (src_v, src_hbm), (mask_ref, mask_hbm)),
                   small_sems.at[pl.ds(9, 3)])
    begin(out[:2])
    mask_ref[...] = own_mask(src, local[7:8, :], sel)
    out[2].start()
    finished(narrow + [places])
    one = (iota((B, KG * B), 1) & (B - 1)) == iota((B, KG * B), 0)
    at = iota((B, KG * B), 1) >> 6
    none = jnp.zeros((B, KG * B), BF16)
    for m in range(BACK):
        row = m if m < HALF else m + HALF
        put = [jnp.where(one & (at == places_ref[1 + q, row]), 1.0, 0.0).astype(BF16) for q in range(3)]
        put = put[:2] + ([put[2], none] if m % 2 == 0 else [none, put[2]])
        blocks = jnp.concatenate([narrow_ref[m], narrow_ref[BACK + m // 2]], axis=1)
        pool_ref[AFTER + m] = jnp.dot(
            blocks, jnp.concatenate(put, axis=0), preferred_element_type=F32).astype(BF16)
    wide = pltpu.make_async_copy(pool_ref.at[pl.ds(AFTER, BACK)], after_hbm, small_sems.at[14])
    wide.start()
    finished(out[:1] + loads)
    for u in range(7):
        @pl.when(read(u))
        def _(u=u):
            unit(u).wait()
    for i in range(HALF):
        merge_row(i, i, HALF + i, src_ref, mask_ref, rows_ref, pool_ref, merged_ref)
    own = pool_ref[HALF:FS].reshape(HALF * B, KG * B)
    partial_ref[...] = tn(own, merged_ref[...]).astype(BF16)
    last = pltpu.make_async_copy(partial_ref, out_hbm, small_sems.at[12])
    last.start()
    finished(out[1:] + [wide, last])


def straddle(a_cols_t, local, flags, sel, a_next, pool, parts):
    return call(
        straddle_kernel, "straddle", [HBM] + [ANY] * 9,
        [((KG * B, 8 * B), BF16), ((8, 128), jnp.int32), ((PAD, 8 * B), F32),
         ((BACK, B, KG * B), BF16)],
        [
            pltpu.VMEM((7, ROWS), jnp.int32),
            pltpu.VMEM((8, ROWS), F32),
            pltpu.SMEM((8, 128), jnp.int32),
            pltpu.VMEM((PAD, ROWS), BF16),
            pltpu.VMEM((POOL, B, KG * B), BF16),
            pltpu.VMEM((HALF, B, 8 * B), BF16),
            pltpu.VMEM((3, 16, KG * B), BF16),
            pltpu.VMEM((16, 128), BF16),
            pltpu.VMEM((NARROW, B, 128), BF16),
            pltpu.VMEM((HALF * B, 8 * B), BF16),
            pltpu.VMEM((KG * B, 8 * B), BF16),
            pltpu.VMEM((PAD, 8 * B), F32),
            pltpu.VMEM((8, 128), jnp.int32),
            pltpu.SMEM((8, 128), jnp.int32),
            pltpu.VMEM((16, 128), jnp.int32),
            pltpu.SMEM((16, 128), jnp.int32),
            pltpu.SemaphoreType.DMA((4, QUARTERS)),
            pltpu.SemaphoreType.DMA((7,)),
            pltpu.SemaphoreType.DMA((15,)),
        ],
        600_000_000, 6_000_000, 16,
    )(a_cols_t, local, flags, sel, a_next, pool, *parts)


def sets_kernel(src_hbm, flags_hbm, places_hbm, mask_hbm, a_rows_hbm, pool_hbm, *refs):
    *parts, after_hbm = refs[:4]
    (_, out_hbm, first_hbm, src_ref, flag_ref, place_ref, mask_ref, first_ref, pool_ref, rows_ref,
     blocks_ref, merged_ref, small_sems, sems, row_sems, out_sems) = refs[4:]
    small = load_all(((flags_hbm, flag_ref), (src_hbm, src_ref), (places_hbm, place_ref),
                      (mask_hbm, mask_ref)), small_sems)
    begin(small)
    loads = pool_copies(parts, pool_ref, sems) + [
        pltpu.make_async_copy(pool_hbm, pool_ref.at[pl.ds(0, ROWS)], small_sems.at[4]),
        pltpu.make_async_copy(after_hbm, pool_ref.at[pl.ds(AFTER, BACK)], sems.at[3, 0])]

    def fetch(s):
        rows = pl.ds(s * FS, FS)
        return pltpu.make_async_copy(a_rows_hbm.at[rows], rows_ref.at[rows], row_sems.at[s])

    def store(s):
        rows = pl.ds(s * KG, KG)
        return pltpu.make_async_copy(blocks_ref.at[rows], out_hbm.at[rows], out_sems.at[s])

    def here(s):
        return flag_ref[s + 1, 0] != 0

    fetch(0).start()
    begin(loads)
    finished(small)
    for s in range(1, SETS):
        @pl.when(here(s))
        def _(s=s):
            fetch(s).start()
    fetch(0).wait()
    finished(loads)
    for i in range(HALF):
        merge_row(i, i, i, src_ref, mask_ref, rows_ref, pool_ref, merged_ref)
    own = pool_ref[:HALF].reshape(HALF * B, KG * B)
    first_ref[...] = tn(own, merged_ref[:HALF * B, :])
    first = pltpu.make_async_copy(first_ref, first_hbm, small_sems.at[5])
    first.start()

    def work(s, carry):
        @pl.when(here(s))
        def _():
            fetch(s).wait()
            one_set(s, src_ref, mask_ref, rows_ref, pool_ref, merged_ref, place_ref, blocks_ref)
            store(s).start()
        return carry

    lax.fori_loop(1, SETS, work, 0)

    def end(s, carry):
        @pl.when(here(s))
        def _():
            store(s).wait()
        return carry

    lax.fori_loop(1, SETS, end, 0)
    first.wait()


def sets(src, flags, places, mask, a_rows, pool, parts, whole):
    return call(
        sets_kernel, "sets", [ANY] * 11,
        [((SETS * KG, 8, B, B), BF16), ((KG * B, 8 * B), F32)],
        [
            pltpu.SMEM((8, 128), jnp.int32),
            pltpu.SMEM((8, 128), jnp.int32),
            pltpu.SMEM((8, 128), jnp.int32),
            pltpu.VMEM((PAD, 8 * B), F32),
            pltpu.VMEM((KG * B, 8 * B), F32),
            pltpu.VMEM((POOL, B, KG * B), BF16),
            pltpu.VMEM((ROWS, B, 8 * B), BF16),
            pltpu.VMEM((SETS * KG, 8, B, B), BF16),
            pltpu.VMEM((FS * B, 8 * B), BF16),
            pltpu.SemaphoreType.DMA((6,)),
            pltpu.SemaphoreType.DMA((4, QUARTERS)),
            pltpu.SemaphoreType.DMA((SETS,)),
            pltpu.SemaphoreType.DMA((SETS,)),
        ],
        2_500_000_000, 12_000_000, 48, aliases={10: 0},
    )(src, flags, places, mask, a_rows, pool, *parts, whole)


def finish_kernel(places_hbm, first_hbm, incoming_hbm, _, out_hbm, place_ref, first_ref, incoming_ref,
                  blocks_ref, sems):
    loads = load_all(((places_hbm, place_ref), (first_hbm, first_ref), (incoming_hbm, incoming_ref)),
                     sems)
    begin(loads)
    finished(loads)
    store_blocks(first_ref[...] + incoming_ref[...].astype(F32), 0, place_ref, blocks_ref)
    copy = pltpu.make_async_copy(blocks_ref, out_hbm.at[pl.ds(0, KG)], sems.at[3])
    copy.start()
    copy.wait()


def finish(places, first, incoming, whole):
    return call(
        finish_kernel, "finish", [ANY] * 4, [((SETS * KG, 8, B, B), BF16)],
        [
            pltpu.SMEM((8, 128), jnp.int32),
            pltpu.VMEM((KG * B, 8 * B), F32),
            pltpu.VMEM((KG * B, 8 * B), BF16),
            pltpu.VMEM((KG, 8, B, B), BF16),
            pltpu.SemaphoreType.DMA((4,)),
        ],
        1_000_000, 1_500_000, 6, aliases={3: 0},
    )(places, first, incoming, whole)[0]


def shards(a_blocks, a_cols, p_blocks, p_cols, c_cols):
    cols_t, a_cols_t, c_cols_t = p_cols.T, a_cols.T, c_cols.T
    moves = (("dom", 1), ("dom", -1), ("sub", 1), ("sub", -1))
    pool, *sends = prolong(cols_t, p_blocks.transpose(1, 2, 3, 0))
    parts = [passed_along(rows, axis, step) for rows, (axis, step) in zip(sends, moves)]
    a_rows, a_next, whole, local, flags, sel, places = operator(
        c_cols_t, cols_t, a_cols_t, a_blocks.transpose(1, 2, 3, 0), pool)
    partial, src, mask, after = straddle(a_cols_t, local, flags, sel, a_next, pool, parts)
    incoming = passed_along(partial, "sub", 1)
    whole, first = sets(
        src, flags, places, mask, a_rows, pool, parts[:3] + [after], whole)
    return finish(places, first, incoming, whole)


def solution(mesh):
    spec4 = P(("dom", "sub"), None, None, None)
    spec2 = P(("dom", "sub"), None)
    return jax.shard_map(
        shards, mesh=mesh, in_specs=(spec4, spec2, spec4, spec2, spec2), out_specs=spec4,
        check_vma=False,
    )
```

```python
import jax
import jax.numpy as jnp
from jax import lax
from jax.experimental import pallas as pl
from jax.experimental.pallas import tpu as pltpu
from jax.sharding import PartitionSpec as P

KG = 4
FS = 14
HALF = FS // 2
ROWS = 84
PAD = 88
SETS = 6
B = 64
POOL = ROWS + FS + FS + HALF + HALF + FS
F32 = jnp.float32
BF16 = jnp.bfloat16


def passed_along(block, axis, distance):
    n = lax.axis_size(axis)
    return lax.ppermute(block, axis, [((i - distance) % n, i) for i in range(n)])


def iota(shape, dim):
    return lax.broadcasted_iota(jnp.int32, shape, dim)


QUARTERS = 4
CHUNK = B // QUARTERS
STRIDE = 89
SENDS = (((70, 14),), ((56, 14),), ((7, 7),))
BACK = HALF + FS
NARROW = BACK + (BACK + 1) // 2
AFTER = POOL - BACK
ANY = pl.BlockSpec(memory_space=pl.ANY)
HBM = pl.BlockSpec(memory_space=pltpu.HBM)


def call(kernel, name, ins, outs, scratch, flops, nbytes, vmem, aliases=None, grid=()):
    return pl.pallas_call(
        kernel,
        grid=grid,
        in_specs=ins,
        out_specs=[ANY] * len(outs),
        out_shape=[jax.ShapeDtypeStruct(*shape) for shape in outs],
        scratch_shapes=scratch,
        input_output_aliases=aliases or {},
        compiler_params=pltpu.CompilerParams(vmem_limit_bytes=vmem * 1024 * 1024),
        cost_estimate=pl.CostEstimate(flops=flops, bytes_accessed=nbytes, transcendentals=0),
        name=name,
    )


def devices():
    dom_count, sub_count = lax.axis_size("dom"), lax.axis_size("sub")
    dom, sub = lax.axis_index("dom"), lax.axis_index("sub")

    def number(d, s):
        return lax.rem(d, dom_count) * sub_count + lax.rem(s, sub_count)

    return [number(dom, sub), number(dom + dom_count - 1, sub), number(dom + 1, sub),
            number(dom, sub + sub_count - 1), number(dom, sub + 1)]


def begin(copies):
    for copy in copies:
        copy.start()


def finished(copies):
    for copy in copies:
        copy.wait()


def load_all(pairs, sems):
    return [pltpu.make_async_copy(src, dst, sems.at[n]) for n, (src, dst) in enumerate(pairs)]


def groups(lead, set_base):
    group = (lead >> 2) - set_base
    own = (group >= 0) & (group < SETS)
    return jnp.where(own, jnp.where(group > 0, group + 1, 0), 1)


def to_column(row):
    wide = jnp.broadcast_to(row, (ROWS, ROWS))
    diagonal = iota((ROWS, ROWS), 0) == iota((ROWS, ROWS), 1)
    return jnp.sum(jnp.where(diagonal, wide, 0.0), axis=1, keepdims=True)


def ranks(key):
    order = (key * 128 + iota((1, ROWS), 1)).astype(F32)
    return jnp.sum(jnp.where(to_column(order) < order, 1.0, 0.0), axis=0, keepdims=True)


def selector(rank):
    return jnp.where(rank.astype(jnp.int32) == iota((PAD, ROWS), 0), 1.0, 0.0).astype(BF16)


def sorted_order(sel):
    return nt(iota((16, ROWS), 1).astype(F32).astype(BF16), sel)


def nt(x, y):
    return lax.dot_general(x, y, (((1,), (1,)), ((), ())), preferred_element_type=F32)


def tn(x, y):
    return lax.dot_general(x, y, (((0,), (0,)), ((), ())), preferred_element_type=F32)


def quarter(c):
    return pl.ds(pl.multiple_of(c * CHUNK, CHUNK), CHUNK)


def send_copies(c, pool_ref, send_refs, sems):
    copies = []
    for ref, runs in zip(send_refs, SENDS):
        total = sum(n for _, n in runs)
        done = 0
        for first, n in runs:
            copies.append(pltpu.make_async_copy(
                pool_ref.at[pl.ds(first, n), quarter(c)],
                ref.at[pl.ds(c * total + done, n)],
                sems.at[c, len(copies)],
            ))
            done += n
    return copies


def prolong_kernel(cols_ref, p_ref, pool_hbm, up_hbm, down_hbm, fore_hbm, back_hbm,
                   sel_ref, back_sel_ref, pool_ref, back_ref, ids_ref, back_ids_ref,
                   t0_ref, t1_ref, t2_ref, t3_ref, out_sems, id_sems):
    c = pl.program_id(0)
    sends = (up_hbm, down_hbm, fore_hbm)

    def stores(c):
        whole = pltpu.make_async_copy(
            pool_ref.at[:, quarter(c)], pool_hbm.at[:, quarter(c)], out_sems.at[c, 5])
        rows = pl.ds(c * NARROW, NARROW)
        back = pltpu.make_async_copy(back_ref.at[rows], back_hbm.at[rows], out_sems.at[c, 4])
        return [back] + send_copies(c, pool_ref, sends, out_sems) + [whole]

    id_copies = [pltpu.make_async_copy(ids_ref, ref.at[ref.shape[0] - 1], id_sems.at[n])
                 for n, ref in enumerate(sends)]
    id_copies.append(pltpu.make_async_copy(
        back_ids_ref, back_hbm.at[back_hbm.shape[0] - 1], id_sems.at[3]))

    @pl.when(c == 0)
    def _():
        rank = ranks(groups(cols_ref[0:1, :], devices()[0] * SETS))
        sel = selector(rank)
        sel_ref[...] = sel
        back_rank = jnp.where(rank < 7.0, rank, jnp.where((rank >= 14.0) & (rank < 28.0), rank - 7.0, 99.0))
        back_sel_ref[...] = jnp.where(
            back_rank.astype(jnp.int32) == iota((32, ROWS), 0), 1.0, 0.0).astype(BF16)
        notes = iota((16, ROWS), 1)
        for q in range(3):
            notes = jnp.where(iota((16, ROWS), 0) == q + 1, cols_ref[q:q + 1, :] & 3, notes)
        notes = nt(notes.astype(F32).astype(BF16), sel).astype(BF16)
        ids_ref[...] = jnp.zeros((16, KG * B), BF16)
        ids_ref[:, :PAD] = notes
        back_ids_ref[...] = jnp.zeros((16, 128), BF16)
        back_ids_ref[:, :PAD] = notes
        begin(id_copies)

    sel = sel_ref[...]
    back_sel = back_sel_ref[...]
    place = cols_ref[...] & 3
    weights = [
        [jnp.where(place[q:q + 1, :] == r, 1.0, 0.0).astype(BF16) for q in range(3)]
        for r in range(KG)
    ]
    for b in range(CHUNK):
        x = [p_ref[q, b] for q in range(3)]
        y = [x[0] * w[0] + x[1] * w[1] + x[2] * w[2] for w in weights]
        t = nt(sel, jnp.concatenate(y, axis=0))
        t0_ref[b * STRIDE:b * STRIDE + PAD, :] = t[:, :128]
        t1_ref[b * STRIDE:b * STRIDE + PAD, :] = t[:, 128:]
        t = nt(back_sel, jnp.concatenate(x + [x[2]], axis=0))
        t2_ref[b * 33:b * 33 + 32, :] = t[:, :128]
        t3_ref[b * 33:b * 33 + 32, :] = t[:, 128:]
    left = iota((CHUNK, 128), 1) < B
    for m in range(BACK):
        back_ref[c * NARROW + m] = t2_ref[pl.ds(m, CHUNK, stride=33), :].astype(BF16)
    for m in range(0, BACK, 2):
        back_ref[c * NARROW + BACK + m // 2] = jnp.where(
            left, t3_ref[pl.ds(m, CHUNK, stride=33), :], t3_ref[pl.ds(m + 1, CHUNK, stride=33), :]
        ).astype(BF16)
    for i in range(ROWS):
        pool_ref[i, quarter(c), :] = jnp.concatenate(
            [t[pl.ds(i, CHUNK, stride=STRIDE), :] for t in (t0_ref, t1_ref)], axis=1
        ).astype(BF16)
    begin(stores(c))

    @pl.when(c == QUARTERS - 1)
    def _():
        finished(id_copies)
        for done in range(QUARTERS):
            finished(stores(done))


def prolong(cols_t, p_t):
    def rows(n):
        return (QUARTERS * n + 1, CHUNK, KG * B), BF16

    return call(
        prolong_kernel, "prolong",
        [pl.BlockSpec((3, ROWS), lambda c: (0, 0)),
         pl.BlockSpec((3, CHUNK, B, ROWS), lambda c: (0, c, 0, 0))],
        [((ROWS, B, KG * B), BF16), rows(14), rows(14), rows(7),
         ((QUARTERS * NARROW + 1, CHUNK, 128), BF16)],
        [
            pltpu.VMEM((PAD, ROWS), BF16),
            pltpu.VMEM((32, ROWS), BF16),
            pltpu.VMEM((ROWS, B, KG * B), BF16),
            pltpu.VMEM((QUARTERS * NARROW, CHUNK, 128), BF16),
            pltpu.VMEM((16, KG * B), BF16),
            pltpu.VMEM((16, 128), BF16),
            pltpu.VMEM((CHUNK * STRIDE, 128), F32),
            pltpu.VMEM((CHUNK * STRIDE, 128), F32),
            pltpu.VMEM((CHUNK * 33, 128), F32),
            pltpu.VMEM((CHUNK * 33, 128), F32),
            pltpu.SemaphoreType.DMA((QUARTERS, 6)),
            pltpu.SemaphoreType.DMA((4,)),
        ],
        6_000_000_000, 8_000_000, 56, grid=(QUARTERS,),
    )(cols_t, p_t)


def set_name(slot):
    name = jnp.where(slot < 7, 0.0, 1.0)
    for start, value in ((14, 2.0), (28, 3.0), (42, 4.0), (56, 5.0), (70, 6.0), (84, 7.0),
                         (98, 8.0), (112, 0.0), (119, 1.0), (126, 9.0)):
        name = jnp.where(slot >= start, value, name)
    return name


def own_mask(src, key, sel):
    own = jnp.where(set_name(src) == key, 1.0, 0.0)
    by_row = nt(sel, own.astype(BF16)).astype(BF16)
    spread = jnp.where(iota((8, 8 * B), 1) >> 6 == iota((8, 8 * B), 0), 1.0, 0.0).astype(BF16)
    return jnp.dot(by_row, spread, preferred_element_type=F32)


def sorted_slots(src, sel):
    return nt(jnp.maximum(src, 0.0).astype(BF16), sel).astype(jnp.int32)


def merge_row(i, place, row, src_ref, mask_ref, a_ref, pool_ref, merged_ref):
    index = [src_ref[k, row] for k in range(7)]
    w = jnp.concatenate([pool_ref[j] for j in index] + [pool_ref[index[0]]], axis=0)
    a = a_ref[i]
    mask = jnp.broadcast_to(mask_ref[pl.ds(row, 1), :], a.shape).astype(BF16)
    a_own = a * mask
    both = jnp.concatenate([a_own, a - a_own], axis=0)
    merged = jnp.dot(both, w, preferred_element_type=F32).astype(BF16)
    merged_ref[place * B:place * B + B, :KG * B] = merged[:B]
    merged_ref[place * B:place * B + B, KG * B:] = merged[B:]


def slot_places(c_cols, set_base):
    row = iota(c_cols.shape, 1)
    u = (c_cols & 3) + jnp.where((c_cols >> 2) == set_base + (row >> 2), 0, 4)
    place = jnp.zeros(c_cols.shape, jnp.int32)
    for slot in range(8):
        place = place + jnp.where(u[slot:slot + 1, :] == iota(c_cols.shape, 0), slot, 0)
    return place


def store_blocks(total, first_row, place_ref, out_ref):
    total = total.astype(BF16)
    for r in range(KG):
        for u in range(8):
            out_ref[first_row + r, place_ref[u, first_row + r]] = total[r * B:(r + 1) * B, u * B:(u + 1) * B]


def one_set(s, src_ref, mask_ref, a_ref, pool_ref, merged_ref, place_ref, blocks_ref):
    first = s * FS
    for i in range(FS):
        merge_row(first + i, i, first + i, src_ref, mask_ref, a_ref, pool_ref, merged_ref)
    own = pool_ref[pl.ds(first, FS)].reshape(FS * B, KG * B)
    store_blocks(tn(own, merged_ref[...]), s * KG, place_ref, blocks_ref)


def operator_kernel(c_cols_hbm, cols_hbm, a_cols_hbm, a_hbm, pool_hbm,
                    a_rows_hbm, a_next_hbm, out_hbm, local_hbm, flags_hbm, sel_hbm, places_hbm,
                    c_cols_ref, cols_ref, a_cols_ref, a_ref, rows_ref, pool_ref, blocks_ref, merged_ref,
                    mask_ref, local_ref, sel_ref, order_v, src_v, flag_v, place_v, order_ref, src_ref, flag_s,
                    place_ref, t0, t1, t2, t3, in_sems, sems, keep_sems, out_sems):
    def fetch(c):
        return pltpu.make_async_copy(a_hbm.at[:, quarter(c)], a_ref.at[:, quarter(c)], in_sems.at[c])

    small = load_all(((cols_hbm, cols_ref), (a_cols_hbm, a_cols_ref), (c_cols_hbm, c_cols_ref)), sems)
    begin(small)
    for c in range(QUARTERS):
        fetch(c).start()
    load = pltpu.make_async_copy(pool_hbm, pool_ref, sems.at[3])
    load.start()
    finished(small)

    device = devices()[0]
    set_base = device * SETS
    key = groups(cols_ref[0:1, :], set_base)
    rank = ranks(key)
    sel = selector(rank)
    sel_ref[...] = sel
    order_v[:, :PAD] = sorted_order(sel)[:8].astype(jnp.int32)
    order_v[:, PAD:] = jnp.zeros((8, 128 - PAD), jnp.int32)
    rank = to_column(rank) + 1.0
    row = iota((ROWS, ROWS), 0)
    sources = [
        jnp.sum(jnp.where(a_cols_ref[k:k + 1, :] - device * ROWS == row, rank, 0.0), axis=0,
                keepdims=True) - 1.0
        for k in range(7)
    ]
    src = jnp.concatenate(sources + [sources[0]], axis=0)
    keys = key.astype(F32)
    eight = iota((8, ROWS), 0)
    local_ref[...] = jnp.where(eight < 7, src, keys)
    away = jnp.max(jnp.where(src < 0.0, 1.0, 0.0), axis=0, keepdims=True)
    away = jnp.sum(jnp.where(eight.astype(F32) == keys, away, 0.0), axis=1, keepdims=True)
    name = jnp.where((src >= 0.0) & (keys == 1.0), set_name(src), 99.0)
    read = jnp.zeros((8, ROWS), F32)
    for k in range(7):
        read = read + jnp.where(name[k:k + 1, :] == eight.astype(F32), 1.0, 0.0)
    read = jnp.sum(read, axis=1, keepdims=True)
    flag_v[...] = jnp.where(iota((8, 128), 1) < 64, away, read).astype(jnp.int32)
    src_v[:, :PAD] = sorted_slots(src, sel)
    src_v[:, PAD:] = jnp.zeros((8, 128 - PAD), jnp.int32)
    place_v[:, :SETS * KG] = slot_places(c_cols_ref[...], set_base)
    place_v[:, SETS * KG:] = jnp.zeros((8, 128 - SETS * KG), jnp.int32)
    mask_ref[...] = own_mask(src, keys, sel)
    to_smem = load_all(((order_v, order_ref), (src_v, src_ref), (flag_v, flag_s),
                        (place_v, place_ref), (local_ref, local_hbm), (flag_v, flags_hbm),
                        (sel_ref, sel_hbm), (place_v, places_hbm)),
                       sems.at[pl.ds(4, 8)])
    begin(to_smem)

    def keep(c, s):
        rows = pl.ds(s * FS, FS)
        return pltpu.make_async_copy(
            rows_ref.at[rows, quarter(c)], a_rows_hbm.at[rows, quarter(c)], keep_sems.at[c, s])

    def keep_next(c):
        return pltpu.make_async_copy(
            rows_ref.at[pl.ds(HALF, HALF), quarter(c)], a_next_hbm.at[:, quarter(c)],
            keep_sems.at[c, SETS])

    def later(s):
        return (flag_s[s + 1, 0] != 0) | (s == 0)

    t_refs = (t0, t1, t2, t3)

    def step(c, carry):
        fetch(c).wait()
        for a in range(CHUNK):
            zero = jnp.zeros((B, ROWS), BF16)
            x = [a_ref[k, c * CHUNK + a] for k in range(7)] + [zero]
            for h in range(4):
                pair = jnp.concatenate(x[2 * h:2 * h + 2], axis=0)
                t_refs[h][a * STRIDE:a * STRIDE + ROWS, :] = jnp.transpose(pair).astype(F32)

        @pl.when(c == 0)
        def _():
            finished(to_smem)

        for i in range(ROWS):
            rows_ref[i, quarter(c), :] = jnp.concatenate(
                [t[pl.ds(order_ref[0, i], CHUNK, stride=STRIDE), :] for t in t_refs], axis=1
            ).astype(BF16)

        def store(s, carry):
            @pl.when(later(s))
            def _():
                keep(c, s).start()
            return carry

        keep_next(c).start()
        return lax.fori_loop(0, SETS, store, carry)

    lax.fori_loop(0, QUARTERS, step, 0)
    load.wait()

    def store(s):
        rows = pl.ds(s * KG, KG)
        return pltpu.make_async_copy(blocks_ref.at[rows], out_hbm.at[rows], out_sems.at[s])

    def work(s, carry):
        @pl.when(flag_s[s + 1, 0] == 0)
        def _():
            one_set(s, src_ref, mask_ref, rows_ref, pool_ref, merged_ref, place_ref, blocks_ref)
            store(s).start()
        return carry

    lax.fori_loop(1, SETS, work, 0)

    def end(s, carry):
        @pl.when(later(s))
        def _():
            finished([keep(c, s) for c in range(QUARTERS)])

        @pl.when(jnp.logical_not(later(s)))
        def _():
            store(s).wait()
        return carry

    lax.fori_loop(0, SETS, end, 0)
    finished([keep_next(c) for c in range(QUARTERS)])


def operator(c_cols_t, cols_t, a_cols_t, a_t, pool):
    return call(
        operator_kernel, "operator", [HBM] * 4 + [ANY],
        [((ROWS, B, 8 * B), BF16), ((HALF, B, 8 * B), BF16), ((SETS * KG, 8, B, B), BF16), ((8, ROWS), F32),
         ((8, 128), jnp.int32), ((PAD, ROWS), BF16), ((8, 128), jnp.int32)],
        [
            pltpu.VMEM((8, SETS * KG), jnp.int32),
            pltpu.VMEM((3, ROWS), jnp.int32),
            pltpu.VMEM((7, ROWS), jnp.int32),
            pltpu.VMEM((7, B, B, ROWS), BF16),
            pltpu.VMEM((ROWS, B, 8 * B), BF16),
            pltpu.VMEM((ROWS, B, KG * B), BF16),
            pltpu.VMEM((SETS * KG, 8, B, B), BF16),
            pltpu.VMEM((FS * B, 8 * B), BF16),
            pltpu.VMEM((PAD, 8 * B), F32),
            pltpu.VMEM((8, ROWS), F32),
            pltpu.VMEM((PAD, ROWS), BF16),
            pltpu.VMEM((8, 128), jnp.int32),
            pltpu.VMEM((8, 128), jnp.int32),
            pltpu.VMEM((8, 128), jnp.int32),
            pltpu.VMEM((8, 128), jnp.int32),
            pltpu.SMEM((8, 128), jnp.int32),
            pltpu.SMEM((8, 128), jnp.int32),
            pltpu.SMEM((8, 128), jnp.int32),
            pltpu.SMEM((8, 128), jnp.int32),
        ] + [pltpu.VMEM(((CHUNK + 1) * STRIDE, 128), F32)] * 4 + [
            pltpu.SemaphoreType.DMA((QUARTERS,)),
            pltpu.SemaphoreType.DMA((12,)),
            pltpu.SemaphoreType.DMA((QUARTERS, SETS + 1)),
            pltpu.SemaphoreType.DMA((SETS,)),
        ],
        4_000_000_000, 18_000_000, 53,
    )(c_cols_t, cols_t, a_cols_t, a_t, pool)


def pool_copies(parts, pool_ref, sems):
    copies = []
    start = ROWS
    for n, part in enumerate(parts):
        rows = (part.shape[0] - 1) // QUARTERS
        for c in range(QUARTERS):
            copies.append(pltpu.make_async_copy(
                part.at[pl.ds(c * rows, rows)],
                pool_ref.at[pl.ds(start, rows), pl.ds(c * CHUNK, CHUNK)],
                sems.at[n, c],
            ))
        start += rows
    return copies


def straddle_kernel(a_cols_hbm, local_hbm, flags_hbm, sel_hbm, a_next_hbm, pool_hbm, *refs):
    *parts, back_hbm = refs[:4]
    (out_hbm, src_hbm, mask_hbm, after_hbm, a_cols_ref, local_ref, flag_ref, sel_ref, pool_ref, rows_ref,
     names_ref, back_names_ref, narrow_ref, merged_ref, partial_ref, mask_ref, src_v, src_ref, places_v,
     places_ref, sems, pool_sems, small_sems) = refs[4:]
    small = load_all(
        [(flags_hbm, flag_ref), (a_cols_hbm, a_cols_ref), (local_hbm, local_ref), (sel_hbm, sel_ref)]
        + [(part.at[part.shape[0] - 1], names_ref.at[n]) for n, part in enumerate(parts)]
        + [(back_hbm.at[back_hbm.shape[0] - 1], back_names_ref)], small_sems)
    begin(small)
    loads = pool_copies(parts, pool_ref, sems)
    loads.append(pltpu.make_async_copy(a_next_hbm, rows_ref, small_sems.at[8]))
    narrow = [
        pltpu.make_async_copy(back_hbm.at[pl.ds(c * NARROW, NARROW)],
                              narrow_ref.at[:, pl.ds(c * CHUNK, CHUNK)], sems.at[3, c])
        for c in range(QUARTERS)
    ]
    begin(narrow + loads)
    finished(small)
    places_v[...] = back_names_ref[...].astype(F32).astype(jnp.int32)
    places = pltpu.make_async_copy(places_v, places_ref, small_sems.at[13])
    places.start()
    ids = devices()

    def unit(u):
        first, rows = (0, 7) if u == 0 else (7, 7) if u == 1 else ((u - 1) * FS, FS)
        return pltpu.make_async_copy(
            pool_hbm.at[pl.ds(first, rows)], pool_ref.at[pl.ds(first, rows)], pool_sems.at[u])

    def read(u):
        return (flag_ref[u, 64] != 0) | (u == 1)

    for u in range(7):
        @pl.when(read(u))
        def _(u=u):
            unit(u).start()

    shifts = (((70, 84, 84 - 70),), ((56, 70, 98 - 56),), ((7, 14, 112 - 7),),
              ((0, 7, 119), (14, 28, 126 - 14)))
    near = ((64, 88), (56, 72), (0, 16), (0, 32))
    found = [jnp.zeros((1, ROWS), F32)] * 7
    for n in range(4):
        low, high = near[n]
        name = names_ref[n][:, :128] if n < 3 else back_names_ref[...]
        column = jnp.transpose(name.astype(F32))[low:high, 0:1].astype(jnp.int32)
        row = iota((high - low, 1), 0) + low
        slot = jnp.zeros((high - low, 1), jnp.int32)
        for first, last, shift in shifts[n]:
            slot = jnp.where((row >= first) & (row < last), row + shift + 1, slot)
        column = jnp.where(slot > 0, column + ids[n + 1] * ROWS, -1)
        slot = slot.astype(F32)
        for k in range(7):
            found[k] = found[k] + jnp.sum(
                jnp.where(a_cols_ref[k:k + 1, :] == column, slot, 0.0), axis=0, keepdims=True)
    local = local_ref[...]
    away = jnp.concatenate(found + [found[0]], axis=0) - 1.0
    src = jnp.where(local >= 0.0, local, away)
    src = jnp.where(iota((8, ROWS), 0) < 7, src, jnp.broadcast_to(src[0:1, :], (8, ROWS)))
    sel = sel_ref[...]
    src_v[:, :PAD] = sorted_slots(src, sel)
    src_v[:, PAD:] = jnp.zeros((8, 128 - PAD), jnp.int32)
    out = load_all(((src_v, src_ref), (src_v, src_hbm), (mask_ref, mask_hbm)),
                   small_sems.at[pl.ds(9, 3)])
    begin(out[:2])
    mask_ref[...] = own_mask(src, local[7:8, :], sel)
    out[2].start()
    finished(narrow + [places])
    one = (iota((B, KG * B), 1) & (B - 1)) == iota((B, KG * B), 0)
    at = iota((B, KG * B), 1) >> 6
    none = jnp.zeros((B, KG * B), BF16)
    for m in range(BACK):
        row = m if m < HALF else m + HALF
        put = [jnp.where(one & (at == places_ref[1 + q, row]), 1.0, 0.0).astype(BF16) for q in range(3)]
        put = put[:2] + ([put[2], none] if m % 2 == 0 else [none, put[2]])
        blocks = jnp.concatenate([narrow_ref[m], narrow_ref[BACK + m // 2]], axis=1)
        pool_ref[AFTER + m] = jnp.dot(
            blocks, jnp.concatenate(put, axis=0), preferred_element_type=F32).astype(BF16)
    wide = pltpu.make_async_copy(pool_ref.at[pl.ds(AFTER, BACK)], after_hbm, small_sems.at[14])
    wide.start()
    finished(out[:1] + loads)
    for u in range(7):
        @pl.when(read(u))
        def _(u=u):
            unit(u).wait()
    for i in range(HALF):
        merge_row(i, i, HALF + i, src_ref, mask_ref, rows_ref, pool_ref, merged_ref)
    own = pool_ref[HALF:FS].reshape(HALF * B, KG * B)
    partial_ref[...] = tn(own, merged_ref[...]).astype(BF16)
    last = pltpu.make_async_copy(partial_ref, out_hbm, small_sems.at[12])
    last.start()
    finished(out[1:] + [wide, last])


def straddle(a_cols_t, local, flags, sel, a_next, pool, parts):
    return call(
        straddle_kernel, "straddle", [HBM] + [ANY] * 9,
        [((KG * B, 8 * B), BF16), ((8, 128), jnp.int32), ((PAD, 8 * B), F32),
         ((BACK, B, KG * B), BF16)],
        [
            pltpu.VMEM((7, ROWS), jnp.int32),
            pltpu.VMEM((8, ROWS), F32),
            pltpu.SMEM((8, 128), jnp.int32),
            pltpu.VMEM((PAD, ROWS), BF16),
            pltpu.VMEM((POOL, B, KG * B), BF16),
            pltpu.VMEM((HALF, B, 8 * B), BF16),
            pltpu.VMEM((3, 16, KG * B), BF16),
            pltpu.VMEM((16, 128), BF16),
            pltpu.VMEM((NARROW, B, 128), BF16),
            pltpu.VMEM((HALF * B, 8 * B), BF16),
            pltpu.VMEM((KG * B, 8 * B), BF16),
            pltpu.VMEM((PAD, 8 * B), F32),
            pltpu.VMEM((8, 128), jnp.int32),
            pltpu.SMEM((8, 128), jnp.int32),
            pltpu.VMEM((16, 128), jnp.int32),
            pltpu.SMEM((16, 128), jnp.int32),
            pltpu.SemaphoreType.DMA((4, QUARTERS)),
            pltpu.SemaphoreType.DMA((7,)),
            pltpu.SemaphoreType.DMA((15,)),
        ],
        600_000_000, 6_000_000, 16,
    )(a_cols_t, local, flags, sel, a_next, pool, *parts)


def sets_kernel(src_hbm, flags_hbm, places_hbm, mask_hbm, a_rows_hbm, pool_hbm, *refs):
    *parts, after_hbm = refs[:4]
    (_, out_hbm, first_hbm, src_ref, flag_ref, place_ref, mask_ref, first_ref, pool_ref, rows_ref,
     blocks_ref, merged_ref, small_sems, sems, row_sems, out_sems) = refs[4:]
    small = load_all(((flags_hbm, flag_ref), (src_hbm, src_ref), (places_hbm, place_ref),
                      (mask_hbm, mask_ref)), small_sems)
    begin(small)
    loads = pool_copies(parts, pool_ref, sems) + [
        pltpu.make_async_copy(pool_hbm, pool_ref.at[pl.ds(0, ROWS)], small_sems.at[4]),
        pltpu.make_async_copy(after_hbm, pool_ref.at[pl.ds(AFTER, BACK)], sems.at[3, 0])]

    def fetch(s):
        rows = pl.ds(s * FS, FS)
        return pltpu.make_async_copy(a_rows_hbm.at[rows], rows_ref.at[rows], row_sems.at[s])

    def store(s):
        rows = pl.ds(s * KG, KG)
        return pltpu.make_async_copy(blocks_ref.at[rows], out_hbm.at[rows], out_sems.at[s])

    def here(s):
        return flag_ref[s + 1, 0] != 0

    fetch(0).start()
    begin(loads)
    finished(small)
    for s in range(1, SETS):
        @pl.when(here(s))
        def _(s=s):
            fetch(s).start()
    fetch(0).wait()
    finished(loads)
    for i in range(HALF):
        merge_row(i, i, i, src_ref, mask_ref, rows_ref, pool_ref, merged_ref)
    own = pool_ref[:HALF].reshape(HALF * B, KG * B)
    first_ref[...] = tn(own, merged_ref[:HALF * B, :])
    first = pltpu.make_async_copy(first_ref, first_hbm, small_sems.at[5])
    first.start()

    def work(s, carry):
        @pl.when(here(s))
        def _():
            fetch(s).wait()
            one_set(s, src_ref, mask_ref, rows_ref, pool_ref, merged_ref, place_ref, blocks_ref)
            store(s).start()
        return carry

    lax.fori_loop(1, SETS, work, 0)

    def end(s, carry):
        @pl.when(here(s))
        def _():
            store(s).wait()
        return carry

    lax.fori_loop(1, SETS, end, 0)
    first.wait()


def sets(src, flags, places, mask, a_rows, pool, parts, whole):
    return call(
        sets_kernel, "sets", [ANY] * 11,
        [((SETS * KG, 8, B, B), BF16), ((KG * B, 8 * B), F32)],
        [
            pltpu.SMEM((8, 128), jnp.int32),
            pltpu.SMEM((8, 128), jnp.int32),
            pltpu.SMEM((8, 128), jnp.int32),
            pltpu.VMEM((PAD, 8 * B), F32),
            pltpu.VMEM((KG * B, 8 * B), F32),
            pltpu.VMEM((POOL, B, KG * B), BF16),
            pltpu.VMEM((ROWS, B, 8 * B), BF16),
            pltpu.VMEM((SETS * KG, 8, B, B), BF16),
            pltpu.VMEM((FS * B, 8 * B), BF16),
            pltpu.SemaphoreType.DMA((6,)),
            pltpu.SemaphoreType.DMA((4, QUARTERS)),
            pltpu.SemaphoreType.DMA((SETS,)),
            pltpu.SemaphoreType.DMA((SETS,)),
        ],
        2_500_000_000, 12_000_000, 48, aliases={10: 0},
    )(src, flags, places, mask, a_rows, pool, *parts, whole)


def finish_kernel(places_hbm, first_hbm, incoming_hbm, _, out_hbm, place_ref, first_ref, incoming_ref,
                  blocks_ref, sems):
    loads = load_all(((places_hbm, place_ref), (first_hbm, first_ref), (incoming_hbm, incoming_ref)),
                     sems)
    begin(loads)
    finished(loads)
    store_blocks(first_ref[...] + incoming_ref[...].astype(F32), 0, place_ref, blocks_ref)
    copy = pltpu.make_async_copy(blocks_ref, out_hbm.at[pl.ds(0, KG)], sems.at[3])
    copy.start()
    copy.wait()


def finish(places, first, incoming, whole):
    return call(
        finish_kernel, "finish", [ANY] * 4, [((SETS * KG, 8, B, B), BF16)],
        [
            pltpu.SMEM((8, 128), jnp.int32),
            pltpu.VMEM((KG * B, 8 * B), F32),
            pltpu.VMEM((KG * B, 8 * B), BF16),
            pltpu.VMEM((KG, 8, B, B), BF16),
            pltpu.SemaphoreType.DMA((4,)),
        ],
        1_000_000, 1_500_000, 6, aliases={3: 0},
    )(places, first, incoming, whole)[0]


def shards(a_blocks, a_cols, p_blocks, p_cols, c_cols):
    cols_t, a_cols_t, c_cols_t = p_cols.T, a_cols.T, c_cols.T
    moves = (("dom", 1), ("dom", -1), ("sub", 1), ("sub", -1))
    pool, *sends = prolong(cols_t, p_blocks.transpose(1, 2, 3, 0))
    parts = [passed_along(rows, axis, step) for rows, (axis, step) in zip(sends, moves)]
    a_rows, a_next, whole, local, flags, sel, places = operator(
        c_cols_t, cols_t, a_cols_t, a_blocks.transpose(1, 2, 3, 0), pool)
    partial, src, mask, after = straddle(a_cols_t, local, flags, sel, a_next, pool, parts)
    incoming = passed_along(partial, "sub", 1)
    whole, first = sets(
        src, flags, places, mask, a_rows, pool, parts[:3] + [after], whole)
    return finish(places, first, incoming, whole)


def solution(mesh):
    spec4 = P(("dom", "sub"), None, None, None)
    spec2 = P(("dom", "sub"), None)
    return jax.shard_map(
        shards, mesh=mesh, in_specs=(spec4, spec2, spec4, spec2, spec2), out_specs=spec4,
        check_vma=False,
    )
```
